32 devices in a mesh: light: 4 (over y, x), view: 8 (over z, core).
Axes of the slice: x: 2, y: 2, z: 4, core: 2. Of those that a mesh axis runs over, the one named last changes fastest.
Arguments:
- density: float32 [64, 256, 4096], P('view', 'light'), may hold values from 0 to 1
- tables: float32 [8, 4, 16], replicated, may hold values from 0.2 to 2
- table_index: int32 [4, 8], P('light', 'view'), may hold values from 0 to 7
- light_code: int32 [4], replicated, may hold values from -1 to 1, as said below
- light_tint: float32 [4, 3], replicated, may hold values from 0.25 to 1
Outputs:
- image: float32 [4, 256, 4096], P(None, ('light', 'view'))
The draws below stay inside these ranges and needn't reach their ends.
Inputs may be any that keep to these rules, and one draw needn't show every extreme that they name: `light_code`: each of -1, 0 and 1 occurs.
All inputs are finite; a program needn't handle non-finite values.
Results may differ from the reference program's by a relative error of at most 0.0003.
Values sent between devices are 32-bit elements; how exact they have to be, the bound alone decides.
No kernel may reach another device: no remote copies, remote signals or barrier semaphores. Data moves between devices by JAX's collectives and lax.ppermute only.
A program may use at most 256 MiB of HBM per device.

```python
import math
import jax
import jax.numpy as jnp
from jax import lax

A_DEV = 64
B_DEV = 8
COLS = 4096
LIGHTS = 4
TABLES = 8
KNOTS = 16
NA = 256
NB = 64
N_LIGHT = 4
N_VIEW = 8


def draw_light_code(key, part):
    extra = jax.random.randint(jax.random.fold_in(key, 7), (LIGHTS - 3,), -1, 2, dtype=jnp.int32)
    base = jnp.concatenate([jnp.array([-1, 0, 1], dtype=jnp.int32), extra])
    return jax.random.permutation(jax.random.fold_in(key, 11), base)


def touch_ends(drawn, stream_key, least, largest):
    extent = drawn.shape
    index_at = [jax.random.randint(jax.random.fold_in(stream_key, axis), (), 0, extent[axis]) for axis in range(len(extent))]
    drawn = drawn.at[tuple(index_at)].set(least)
    longest = extent.index(max(extent))
    index_at[longest] = (index_at[longest] + 1) % extent[longest]
    return drawn.at[tuple(index_at)].set(largest)


def block_levels(key, extent, pieces, least, largest):
    gain, own = 1.0, jax.random.fold_in(key, 6)
    for position, parts in pieces:
        draws = jnp.exp(jax.random.uniform(jax.random.fold_in(own, position), (parts,), jnp.float32, least / len(pieces), largest / len(pieces)))
        gain = gain * jnp.repeat(draws, extent[position] // parts).reshape([-1 if axis == position else 1 for axis in range(len(extent))])
    return gain


def setup_inputs(seed: int = 0) -> dict:
    splits = jax.random.split(jax.random.key(seed), 6)
    density = jnp.clip(1.0 * jax.random.uniform(splits[0], (NB, NA, COLS), jnp.float32) ** block_levels(splits[0], (NB, NA, COLS), ((0, 8), (1, 4)), -0.2, 0.2), 0.0, 1.0)
    tables = jnp.clip(jax.random.uniform(splits[1], (TABLES, 4, KNOTS), jnp.float32, 0.2, 2.0), 0.2, 2.0)
    table_index = touch_ends(jax.random.randint(splits[2], (N_LIGHT, N_VIEW), 0, TABLES), jax.random.fold_in(splits[2], 1), 0, TABLES - 1).astype(jnp.int32)
    light_code = draw_light_code(jax.random.fold_in(splits[5], 71), 0)
    light_tint = jnp.clip(jnp.exp(jax.random.uniform(splits[4], (LIGHTS, 3), jnp.float32, math.log(0.25), math.log(1.0))), 0.25, 1.0)
    return dict(density=density, tables=tables, table_index=table_index, light_code=light_code, light_tint=light_tint)


blur_side = 0.25


def table_values(field, table):
    knot_count = table.shape[1]
    scaled = field * (knot_count - 1)
    floor_at = jnp.clip(jnp.floor(scaled), 0.0, knot_count - 2.0)
    fraction = scaled - floor_at
    shape_tail = (1,) * field.ndim
    result = jnp.zeros((table.shape[0],) + field.shape, jnp.float32)
    for knot_at in range(knot_count - 1):
        left_value = table[:, knot_at].reshape((-1,) + shape_tail)
        right_value = table[:, knot_at + 1].reshape((-1,) + shape_tail)
        value_here = left_value * (1.0 - fraction[None]) + right_value * fraction[None]
        result = jnp.where((floor_at == knot_at)[None], value_here, result)
    return result


def cone_blur(fronts, codes):
    width = fronts.shape[-1]
    padded = jnp.pad(fronts, ((0, 0), (0, 0), (2, 2)))
    offsets = jnp.arange(-2, 3, dtype=jnp.int32)
    code_col = codes[:, None]
    basis = jnp.where(offsets[None] == code_col, 1.0 - 2.0 * blur_side, 0.0) + jnp.where(jnp.abs(offsets[None] - code_col) == 1, blur_side, 0.0)
    total = jnp.zeros_like(fronts)
    for shift_idx in range(5):
        shift_by = shift_idx - 2
        moved = padded[:, :, 2 - shift_by:2 - shift_by + width]
        total = total + basis[:, shift_idx][:, None, None] * moved
    return total


def reference(density, tables, table_index, light_code, light_tint):
    volume = density.reshape(N_VIEW, B_DEV, NA, COLS)

    def brick(carry, inputs):
        rgb_acc, clear_acc = carry
        slab, row_tables = inputs
        front = jnp.ones((LIGHTS, B_DEV, COLS), jnp.float32)
        rgb_parts = []
        clear_parts = []
        for light_brick in range(N_LIGHT):
            cells = slab[:, light_brick * A_DEV:(light_brick + 1) * A_DEV]
            props = table_values(cells, tables[row_tables[light_brick]])
            sigma = props[0]
            color = props[1:]
            optical = sigma / NA
            before = jnp.cumsum(optical, axis=1) - optical
            shadow = jnp.exp(-before)
            lighting = jnp.einsum('lk,lbc->kbc', light_tint, front, precision=lax.Precision.HIGHEST)
            view_depth = sigma / NB
            view_before = jnp.cumsum(view_depth, axis=0) - view_depth
            weight = jnp.exp(-view_before) * (1.0 - jnp.exp(-view_depth)) * shadow
            rgb_parts.append(jnp.sum(weight[None] * color * lighting[:, :, None, :], axis=1))
            clear_parts.append(jnp.exp(-jnp.sum(view_depth, axis=0)))
            front = cone_blur(front * jnp.exp(-jnp.sum(optical, axis=1))[None], light_code)
        rgb_brick = jnp.concatenate(rgb_parts, axis=1)
        clear_brick = jnp.concatenate(clear_parts, axis=0)
        rgb_acc = rgb_acc + clear_acc[None] * rgb_brick
        clear_acc = clear_acc * clear_brick
        return (rgb_acc, clear_acc), None

    start = (jnp.zeros((3, NA, COLS), jnp.float32), jnp.ones((NA, COLS), jnp.float32))
    (rgb_acc, clear_acc), unused = lax.scan(brick, start, (volume, table_index.T))
    return jnp.concatenate([rgb_acc, clear_acc[None]], axis=0)
```

```python
import functools
import math

import jax
import jax.numpy as jnp
from jax import lax
from jax.experimental import pallas as pl
from jax.experimental.pallas import tpu as pltpu
from jax.sharding import PartitionSpec as P

LANE = 128
SUB = 8
DRIFTS = (-1, 0, 1)
VMEM_LIMIT = 48 * 2**20
F32 = jnp.float32


def params():
    return pltpu.CompilerParams(vmem_limit_bytes=VMEM_LIMIT)


def bit_reversed(value, bits):
    return sum((value >> at & 1) << bits - 1 - at for at in range(bits))


def rows_of(table, index):
    return jnp.take_along_axis(table, index, axis=0, mode="promise_in_bounds")


def fill_coefficients(which, tables_ref, coef, sigma_scale, properties):
    rows = tables_ref[which]
    knots = rows.shape[1]
    at_row = lax.broadcasted_iota(jnp.int32, (2 * SUB, knots), 0)
    at_col = lax.broadcasted_iota(jnp.int32, (2 * SUB, knots), 1)
    left_at = jnp.minimum(at_row, knots - 2)
    for q in range(properties):
        row = jnp.broadcast_to(rows[q : q + 1], (2 * SUB, knots))
        left = jnp.sum(jnp.where(at_col == left_at, row, 0.0), axis=1, keepdims=True)
        right = jnp.sum(jnp.where(at_col == left_at + 1, row, 0.0), axis=1, keepdims=True)
        step = right - left
        start = left - step * left_at[:, :1].astype(F32)
        scale = sigma_scale if q == 0 else 1.0
        start = jnp.broadcast_to(start * scale, (2 * SUB, LANE))
        step = jnp.broadcast_to(step * (scale * (knots - 1)), (2 * SUB, LANE))
        coef[4 * q] = start[:SUB]
        coef[4 * q + 1] = start[SUB:]
        coef[4 * q + 2] = step[:SUB]
        coef[4 * q + 3] = step[SUB:]


def place_of(cells, knots):
    knot = (cells * (knots - 1.0)).astype(jnp.int32)
    return knot & (SUB - 1), knot >= SUB


def value_at(coef, q, place, cells):
    low, high = place
    start = jnp.where(high, rows_of(coef[4 * q + 1], low), rows_of(coef[4 * q], low))
    step = jnp.where(high, rows_of(coef[4 * q + 3], low), rows_of(coef[4 * q + 2], low))
    return start + step * cells


def fetch_tile(density_ref, buffer, sems, first, tile):
    columns = pl.ds(pl.multiple_of(first + tile * LANE, LANE), LANE)
    return pltpu.make_async_copy(density_ref.at[:, :, columns], buffer.at[tile], sems.at[tile])


def sums_kernel(sigma_scale, ratio, first, bits, split, index_ref, tables_ref, density_ref, *rest):
    if split:
        leaving_ref, send_ref, keep_ref, coef, buffer, clear, sems = rest
    else:
        leaving_ref, coef, buffer, sems = rest
    tiles, layers, slices, _ = buffer.shape
    knots = tables_ref.shape[2]

    @pl.loop(0, tiles)
    def _(tile):
        fetch_tile(density_ref, buffer, sems, first, tile).start()

    fill_coefficients(index_ref[0, 0], tables_ref, coef, sigma_scale, 1)
    mine = lax.axis_index("view") & 1 if split else 0
    half = (1 << bits) // 2

    @pl.loop(0, tiles)
    def _(tile):
        fetch_tile(density_ref, buffer, sems, first, tile).wait()
        down = [jnp.zeros((SUB, LANE), F32) for _ in range(layers)]
        for block in range(slices // SUB):
            through = jnp.zeros((SUB, LANE), F32)
            for b in range(layers):
                cells = buffer[tile, b, block * SUB : block * SUB + SUB]
                sigma = value_at(coef, 0, place_of(cells, knots), cells)
                through = through + sigma
                down[b] = down[b] + sigma
            if split:
                clear[block] = jnp.exp2(through)
        columns = pl.ds(pl.multiple_of(tile * LANE, LANE), LANE)
        for b in range(layers):
            leaving_ref[b : b + 1, columns] = jnp.exp2(
                jnp.sum(down[b], axis=0, keepdims=True) * ratio
            )
        if split:
            for q in range(half):
                octet = 2 * bit_reversed(q, bits - 1)
                send_ref[q, tile] = clear[octet + 1 - mine]
                keep_ref[q, tile] = clear[octet + mine]


def fill_lighting(pieces, brick_refs, code_ref, tint_ref, lighting, first, total):
    layers, width = lighting.shape[1:]
    wide = width + 2 * LANE
    place = lax.broadcasted_iota(jnp.int32, (layers, wide), 1) + (first - LANE)
    inside = jnp.logical_and(place >= 0, place < total).astype(F32)
    mine = lax.axis_index("light")
    fronts = [inside] * len(DRIFTS)
    for apart in range(len(brick_refs), 0, -1):
        parts, at = [], first - LANE
        if at < 0:
            parts.append(jnp.zeros((layers, -at), F32))
            at = 0
        for (low, high), ref in zip(pieces, brick_refs[apart - 1]):
            stop = min(high, first + width + LANE)
            if at < stop and at >= low:
                parts.append(ref[:, at - low : stop - low])
                at = stop
        if at < first + width + LANE:
            parts.append(jnp.zeros((layers, first + width + LANE - at), F32))
        leaving = jnp.concatenate(parts, axis=1)
        active = mine >= apart
        result = []
        shared = None
        for drift, front in zip(DRIFTS, fronts):
            if shared is None or apart < len(brick_refs):
                row = front * leaving
                shared = 0.5 * row + 0.25 * (pltpu.roll(row, 1, 1) + pltpu.roll(row, wide - 1, 1))
            moved = shared if drift == 0 else pltpu.roll(shared, drift % wide, 1)
            result.append(jnp.where(active, moved * inside, front))
        fronts = result
    for k in range(lighting.shape[0]):
        shade = jnp.zeros((layers, wide), F32)
        for drift, front in zip(DRIFTS, fronts):
            tint = 0.0
            for light in range(tint_ref.shape[0]):
                tint = tint + jnp.where(code_ref[light] == drift, tint_ref[light, k], 0.0)
            shade = shade + tint * front
        lighting[k] = shade[:, LANE : LANE + width]


def shade_kernel(
    sigma_scale, ratio, first, total, bits, pieces, far, whole_out,
    index_ref, code_ref, tint_ref, tables_ref, density_ref, *rest,
):
    brick_refs = [rest[at * len(pieces) : (at + 1) * len(pieces)] for at in range(far)]
    rest = rest[far * len(pieces) :]
    if whole_out:
        out_ref, coef, buffer, lighting, sums, sems = rest
    else:
        send_ref, keep_ref, coef, buffer, lighting, sums, sems = rest
    tiles, layers, slices, _ = buffer.shape
    knots = tables_ref.shape[2]
    steps = slices // SUB
    channels = lighting.shape[0]

    @pl.loop(0, tiles)
    def _(tile):
        fetch_tile(density_ref, buffer, sems, first, tile).start()

    fill_coefficients(index_ref[0, 0], tables_ref, coef, sigma_scale, tables_ref.shape[1])
    fill_lighting(pieces, brick_refs, code_ref, tint_ref, lighting, first, total)
    mine = lax.axis_index("view") & 1
    sublane = lax.broadcasted_iota(jnp.int32, (SUB, LANE), 0)

    @pl.loop(0, tiles)
    def _(tile):
        fetch_tile(density_ref, buffer, sems, first, tile).wait()
        columns = pl.ds(pl.multiple_of(tile * LANE, LANE), LANE)
        ahead = [None] * steps
        for b in range(layers):
            lit = [
                jnp.broadcast_to(lighting[k, b : b + 1, columns], (SUB, LANE))
                for k in range(channels)
            ]
            cells, places, sigma = [], [], []
            for j in range(steps):
                cells.append(buffer[tile, b, pl.ds(j, SUB, stride=steps), :])
                places.append(place_of(cells[j], knots))
                sigma.append(value_at(coef, 0, places[j], cells[j]))
            before, running = [], None
            for j in range(steps):
                before.append(running)
                running = sigma[j] if running is None else running + sigma[j]
            earlier = running
            for hop in (1, 2, 4):
                earlier = earlier + jnp.where(sublane >= hop, pltpu.roll(earlier, hop, 0), 0.0)
            earlier = earlier - running
            for j in range(steps):
                inside = earlier if j == 0 else earlier + before[j]
                shadow = jnp.exp2(inside * ratio)
                passed = jnp.exp2(sigma[j])
                if b == 0:
                    after = passed
                    weight = (1.0 - passed) * shadow
                else:
                    after = ahead[j] * passed
                    weight = (ahead[j] - after) * shadow
                ahead[j] = after
                rows = pl.ds(j * SUB, SUB)
                for k in range(channels):
                    term = value_at(coef, k + 1, places[j], cells[j]) * (weight * lit[k])
                    if b == 0:
                        sums[k, rows] = term
                    else:
                        sums[k, rows] = sums[k, rows] + term
        if whole_out:
            for j in range(steps):
                sums[channels, pl.ds(j * SUB, SUB)] = ahead[j]
            for octet in range(SUB):
                for k in range(channels + 1):
                    for part in range(steps // SUB):
                        out_ref[k, tile, pl.ds(octet * steps + part * SUB, SUB)] = sums[
                            k, pl.ds(part * SUB * SUB + octet, SUB, stride=SUB), :
                        ]
        else:
            for q in range(1 << bits - 1):
                octet = 2 * bit_reversed(q, bits - 1)
                for k in range(channels):
                    send_ref[q, k, tile] = sums[k, pl.ds(octet + 1 - mine, SUB, stride=SUB), :]
                    keep_ref[q, k, tile] = sums[k, pl.ds(octet + mine, SUB, stride=SUB), :]


VMEM = functools.partial(pl.BlockSpec, memory_space=pltpu.VMEM)
SMEM = functools.partial(pl.BlockSpec, memory_space=pltpu.SMEM)
ANY = functools.partial(pl.BlockSpec, memory_space=pl.ANY)


def shape(*dims):
    return jax.ShapeDtypeStruct(dims, F32)


def cost(density, columns, per_cell):
    cells = density.shape[0] * density.shape[1] * columns
    return pl.CostEstimate(flops=cells * per_cell, bytes_accessed=4 * cells, transcendentals=0)


def sums(density, tables, index, low, high, sigma_scale, ratio, bits, split):
    layers, slices, _ = density.shape
    tiles = (high - low) // LANE
    half = (1 << bits) // 2
    outs = [shape(layers, high - low)]
    scratch = [pltpu.VMEM((4, SUB, LANE), F32), pltpu.VMEM((tiles, layers, slices, LANE), F32)]
    if split:
        outs += [shape(half, tiles, SUB, LANE)] * 2
        scratch.append(pltpu.VMEM((slices // SUB, SUB, LANE), F32))
    scratch.append(pltpu.SemaphoreType.DMA((tiles,)))
    return pl.pallas_call(
        functools.partial(sums_kernel, sigma_scale, ratio, low, bits, split),
        in_specs=[SMEM(), VMEM(), ANY()],
        out_specs=[VMEM()] * len(outs),
        out_shape=outs,
        scratch_shapes=scratch,
        compiler_params=params(),
        cost_estimate=cost(density, high - low, 16),
        name="sums",
    )(index, tables, density)


def shade(density, tables, index, code, tint, bricks, pieces, low, high, sigma_scale, ratio, bits, whole_out):
    layers, slices, total = density.shape
    channels = tint.shape[1]
    tiles = (high - low) // LANE
    half = (1 << bits) // 2
    if whole_out:
        outs = [shape(channels + 1, tiles, slices, LANE)]
    else:
        outs = [shape(half, channels, tiles, SUB, LANE)] * 2
    used = [at for at, (start, stop) in enumerate(pieces) if start < high + LANE and stop > low - LANE]
    operands = [rows[at] for rows in bricks for at in used]
    return pl.pallas_call(
        functools.partial(
            shade_kernel, sigma_scale, ratio, low, total, bits,
            tuple(pieces[at] for at in used), len(bricks), whole_out,
        ),
        in_specs=[SMEM()] * 3 + [VMEM(), ANY()] + [VMEM()] * len(operands),
        out_specs=[VMEM()] * len(outs),
        out_shape=outs,
        scratch_shapes=[
            pltpu.VMEM((4 * tables.shape[1], SUB, LANE), F32),
            pltpu.VMEM((tiles, layers, slices, LANE), F32),
            pltpu.VMEM((channels, layers, high - low), F32),
            pltpu.VMEM((channels + 1, slices, LANE), F32),
            pltpu.SemaphoreType.DMA((tiles,)),
        ],
        compiler_params=params(),
        cost_estimate=cost(density, high - low, 60),
        name="shade",
    )(index, code, tint, tables, density, *operands)


def merge_clear_kernel(bit, own_ref, other_ref, send_ref, keep_ref):
    half = send_ref.shape[0]
    mine = lax.axis_index("view") >> bit + 1 & 1
    for at in range(half):
        there, here = (1 - mine) * half + at, mine * half + at
        send_ref[at] = own_ref[there] * other_ref[there]
        keep_ref[at] = own_ref[here] * other_ref[here]


def merge_clear(own, other, bit):
    half = shape(own.shape[0] // 2, *own.shape[1:])
    return pl.pallas_call(
        functools.partial(merge_clear_kernel, bit),
        in_specs=[VMEM()] * 2,
        out_specs=[VMEM()] * 2,
        out_shape=[half] * 2,
        compiler_params=params(),
        name="merge_clear",
    )(own, other)


def merge_kernel(bit, own_ref, other_ref, own_clear_ref, other_clear_ref, send_ref, keep_ref):
    half = send_ref.shape[0]
    me = lax.axis_index("view")
    mine = me >> bit + 1 & 1

    def merged(front_ref, back_ref, clear_ref):
        for at in range(half):
            for to_ref, side in ((send_ref, 1 - mine), (keep_ref, mine)):
                source = side * half + at
                clear = clear_ref[source]
                for k in range(send_ref.shape[1]):
                    to_ref[at, k] = front_ref[source, k] + clear * back_ref[source, k]

    upper = me >> bit & 1 == 1

    @pl.when(upper)
    def _():
        merged(other_ref, own_ref, other_clear_ref)

    @pl.when(jnp.logical_not(upper))
    def _():
        merged(own_ref, other_ref, own_clear_ref)


def unit_of(low, high):
    return math.gcd(low // LANE, (high - low) // LANE)


def merge(own, other, own_clear, other_clear, bit, low, high):
    count, channels, tiles = own.shape[:3]
    unit = unit_of(low, high)
    start = low // LANE // unit
    half = count // 2
    data = lambda n: pl.BlockSpec((n, channels, unit, SUB, LANE), lambda i: (0, 0, i, 0, 0))
    clear = pl.BlockSpec((count, unit, SUB, LANE), lambda i: (0, start + i, 0, 0))
    return pl.pallas_call(
        functools.partial(merge_kernel, bit),
        grid=(tiles // unit,),
        in_specs=[data(count)] * 2 + [clear] * 2,
        out_specs=[data(half)] * 2,
        out_shape=[shape(half, *own.shape[1:])] * 2,
        compiler_params=params(),
        name="merge",
    )(own, other, own_clear, other_clear)


def last_kernel(bit, own_ref, other_ref, own_clear_ref, other_clear_ref, *rest):
    image_ref = rest[-1]
    channels, tiles = own_ref.shape[1:3]

    def merged(front_ref, back_ref, clear_ref):
        for tile in range(tiles):
            columns = slice(tile * LANE, tile * LANE + LANE)
            clear = clear_ref[0, tile]
            for k in range(channels):
                image_ref[k, :, columns] = front_ref[0, k, tile] + clear * back_ref[0, k, tile]
            image_ref[channels, :, columns] = own_clear_ref[0, tile] * other_clear_ref[0, tile]

    upper = lax.axis_index("view") >> bit & 1 == 1

    @pl.when(upper)
    def _():
        merged(other_ref, own_ref, other_clear_ref)

    @pl.when(jnp.logical_not(upper))
    def _():
        merged(own_ref, other_ref, own_clear_ref)


def last(own, other, own_clear, other_clear, bit, low, high, total, image):
    _, channels, tiles = own.shape[:3]
    unit = unit_of(low, high)
    start = low // LANE // unit
    data = pl.BlockSpec((1, channels, unit, SUB, LANE), lambda i: (0, 0, i, 0, 0))
    clear = pl.BlockSpec((1, unit, SUB, LANE), lambda i: (0, start + i, 0, 0))
    before = [] if image is None else [image]
    return pl.pallas_call(
        functools.partial(last_kernel, bit),
        grid=(tiles // unit,),
        in_specs=[data] * 2 + [clear] * 2 + [ANY()] * len(before),
        out_specs=pl.BlockSpec((channels + 1, SUB, unit * LANE), lambda i: (0, 0, start + i)),
        out_shape=shape(channels + 1, SUB, total),
        input_output_aliases={4: 0} if before else {},
        compiler_params=params(),
        name="last",
    )(own, other, own_clear, other_clear, *before)


def swap(block, bit):
    count = lax.axis_size("view")
    return lax.ppermute(block, "view", [(at, at ^ 1 << bit) for at in range(count)])


def from_earlier(leaving):
    count = lax.axis_size("light")
    return [
        lax.ppermute(leaving, "light", [(at, at + apart) for at in range(count - apart)])
        for apart in range(1, count)
    ]


def composite_over(front, back):
    clear = front[-1:]
    return jnp.concatenate([front[:-1] + clear * back[:-1], clear * back[-1:]])


def plain(density, tables, table_index, light_code, light_tint, sigma_scale, ratio, bits):
    slices, total = density.shape[1:]
    [leaving] = sums(density, tables, table_index, 0, total, sigma_scale, ratio, 0, False)
    bricks = [[row] for row in from_earlier(leaving)]
    parts = shade(
        density, tables, table_index, light_code, light_tint, bricks, [(0, total)], 0, total,
        sigma_scale, ratio, 0, True,
    )[0]
    rows = slices >> bits
    depth = parts.shape[0]
    current = parts.transpose(0, 2, 1, 3).reshape((depth,) + (2,) * bits + (rows, total))
    current = current.transpose((0,) + tuple(range(bits, 0, -1)) + (bits + 1, bits + 2))
    for bit in range(bits):
        upper = lax.axis_index("view") >> bit & 1 == 1
        first, second = current[:, 0], current[:, 1]
        kept = jnp.where(upper, second, first)
        arrived = swap(jnp.where(upper, first, second), bit)
        current = composite_over(jnp.where(upper, arrived, kept), jnp.where(upper, kept, arrived))
    return current.reshape(depth, rows, total)


LIGHT_CUTS = (0.28125,)
CUTS = (0.25, 0.625)


def ranges(cuts, total):
    ends = [0] + [round(total * cut / LANE) * LANE for cut in cuts] + [total]
    return list(zip(ends[:-1], ends[1:]))


def local(density, tables, table_index, light_code, light_tint):
    layers, slices, total = density.shape
    views = lax.axis_size("view")
    bits = views.bit_length() - 1
    sigma_scale = -math.log2(math.e) / (layers * views)
    ratio = layers * views / (slices * lax.axis_size("light"))
    if views * SUB != slices:
        return plain(
            density, tables, table_index, light_code, light_tint, sigma_scale, ratio, bits
        )
    pieces = ranges(LIGHT_CUTS, total)
    bricks = [[] for _ in range(lax.axis_size("light") - 1)]
    clears = []
    for low, high in pieces:
        leaving, *halves = sums(
            density, tables, table_index, low, high, sigma_scale, ratio, bits, True
        )
        clears.append(halves)
        for rows, row in zip(bricks, from_earlier(leaving)):
            rows.append(row)
    send, keep = (jnp.concatenate(parts, axis=1) for parts in zip(*clears))
    clear = []
    for bit in range(bits):
        clear.append((keep, swap(send, bit)))
        if bit < bits - 1:
            send, keep = merge_clear(*clear[bit], bit)
    image = None
    for low, high in ranges(CUTS, total):
        send, keep = shade(
            density, tables, table_index, light_code, light_tint, bricks, pieces, low, high,
            sigma_scale, ratio, bits, False,
        )
        for bit in range(bits - 1):
            send, keep = merge(keep, swap(send, bit), *clear[bit], bit, low, high)
        bit = bits - 1
        image = last(keep, swap(send, bit), *clear[bit], bit, low, high, total, image)
    return image


def solution(mesh):
    return jax.shard_map(
        local,
        mesh=mesh,
        in_specs=(P("view", "light", None), P(), P("light", "view"), P(), P()),
        out_specs=P(None, ("light", "view"), None),
        check_vma=False,
    )
```

```python
import functools
import math

import jax
import jax.numpy as jnp
from jax import lax
from jax.experimental import pallas as pl
from jax.experimental.pallas import tpu as pltpu
from jax.sharding import PartitionSpec as P

LANE = 128
SUB = 8
DRIFTS = (-1, 0, 1)
VMEM_LIMIT = 24 * 2**20
STREAM_LIMIT = 52 * 2**20
F32 = jnp.float32


def params(limit=VMEM_LIMIT):
    return pltpu.CompilerParams(vmem_limit_bytes=limit)


def bit_reversed(value, bits):
    return sum((value >> at & 1) << bits - 1 - at for at in range(bits))


def rows_of(table, index):
    return jnp.take_along_axis(table, index, axis=0, mode="promise_in_bounds")


def fill_coefficients(which, tables_ref, coef, sigma_scale, properties):
    rows = tables_ref[which]
    knots = rows.shape[1]
    at_row = lax.broadcasted_iota(jnp.int32, (2 * SUB, knots), 0)
    at_col = lax.broadcasted_iota(jnp.int32, (2 * SUB, knots), 1)
    left_at = jnp.minimum(at_row, knots - 2)
    for q in range(properties):
        row = jnp.broadcast_to(rows[q : q + 1], (2 * SUB, knots))
        left = jnp.sum(jnp.where(at_col == left_at, row, 0.0), axis=1, keepdims=True)
        right = jnp.sum(jnp.where(at_col == left_at + 1, row, 0.0), axis=1, keepdims=True)
        step = right - left
        start = left - step * left_at[:, :1].astype(F32)
        scale = sigma_scale if q == 0 else 1.0
        start = jnp.broadcast_to(start * scale, (2 * SUB, LANE))
        step = jnp.broadcast_to(step * (scale * (knots - 1)), (2 * SUB, LANE))
        coef[4 * q] = start[:SUB]
        coef[4 * q + 1] = start[SUB:]
        coef[4 * q + 2] = step[:SUB]
        coef[4 * q + 3] = step[SUB:]


def place_of(cells, knots):
    knot = (cells * (knots - 1.0)).astype(jnp.int32)
    return knot & (SUB - 1), knot >= SUB


def value_at(table, place, cells):
    low, high = place
    start = jnp.where(high, rows_of(table[1], low), rows_of(table[0], low))
    step = jnp.where(high, rows_of(table[3], low), rows_of(table[2], low))
    return start + step * cells


def table_of(coef, q):
    return [coef[4 * q + at] for at in range(4)]


def fetch_tile(density_ref, buffer, sems, first, tile):
    columns = pl.ds(pl.multiple_of(first + tile * LANE, LANE), LANE)
    return pltpu.make_async_copy(density_ref.at[:, :, columns], buffer.at[tile], sems.at[tile])


def sums_kernel(sigma_scale, ratio, first, bits, split, index_ref, tables_ref, density_ref, *rest):
    if split:
        leaving_ref, send_ref, keep_ref, coef, buffer, clear, sems = rest
    else:
        leaving_ref, coef, buffer, sems = rest
    tiles, layers, slices, _ = buffer.shape
    knots = tables_ref.shape[2]

    @pl.loop(0, tiles)
    def _(tile):
        fetch_tile(density_ref, buffer, sems, first, tile).start()

    fill_coefficients(index_ref[0, 0], tables_ref, coef, sigma_scale, 1)
    mine = lax.axis_index("view") & 1 if split else 0
    half = (1 << bits) // 2

    @pl.loop(0, tiles)
    def _(tile):
        fetch_tile(density_ref, buffer, sems, first, tile).wait()
        table = table_of(coef, 0)
        down = [jnp.zeros((SUB, LANE), F32) for _ in range(layers)]
        for block in range(slices // SUB):
            through = jnp.zeros((SUB, LANE), F32)
            for b in range(layers):
                cells = buffer[tile, b, block * SUB : block * SUB + SUB]
                sigma = value_at(table, place_of(cells, knots), cells)
                through = through + sigma
                down[b] = down[b] + sigma
            if split:
                clear[block] = jnp.exp2(through)
        columns = pl.ds(pl.multiple_of(tile * LANE, LANE), LANE)
        for b in range(layers):
            leaving_ref[b : b + 1, columns] = jnp.exp2(
                jnp.sum(down[b], axis=0, keepdims=True) * ratio
            )
        if split:
            for q in range(half):
                octet = 2 * bit_reversed(q, bits - 1)
                send_ref[q, tile] = clear[octet + 1 - mine]
                keep_ref[q, tile] = clear[octet + mine]


def fill_lighting(pieces, brick_refs, code_ref, tint_ref, lighting, first, total):
    layers, width = lighting.shape[1:]
    wide = width + 2 * LANE
    place = lax.broadcasted_iota(jnp.int32, (layers, wide), 1) + (first - LANE)
    inside = jnp.logical_and(place >= 0, place < total).astype(F32)
    mine = lax.axis_index("light")
    fronts = [inside] * len(DRIFTS)
    for apart in range(len(brick_refs), 0, -1):
        parts, at = [], first - LANE
        if at < 0:
            parts.append(jnp.zeros((layers, -at), F32))
            at = 0
        for (low, high), ref in zip(pieces, brick_refs[apart - 1]):
            stop = min(high, first + width + LANE)
            if at < stop and at >= low:
                parts.append(ref[:, at - low : stop - low])
                at = stop
        if at < first + width + LANE:
            parts.append(jnp.zeros((layers, first + width + LANE - at), F32))
        leaving = jnp.concatenate(parts, axis=1)
        active = mine >= apart
        result = []
        shared = None
        for drift, front in zip(DRIFTS, fronts):
            if shared is None or apart < len(brick_refs):
                row = front * leaving
                shared = 0.5 * row + 0.25 * (pltpu.roll(row, 1, 1) + pltpu.roll(row, wide - 1, 1))
            moved = shared if drift == 0 else pltpu.roll(shared, drift % wide, 1)
            result.append(jnp.where(active, moved * inside, front))
        fronts = result
    for k in range(lighting.shape[0]):
        shade = jnp.zeros((layers, wide), F32)
        for drift, front in zip(DRIFTS, fronts):
            tint = 0.0
            for light in range(tint_ref.shape[0]):
                tint = tint + jnp.where(code_ref[light] == drift, tint_ref[light, k], 0.0)
            shade = shade + tint * front
        lighting[k] = shade[:, LANE : LANE + width]


def weights_of(coef, buffer, tile, b, ahead, ratio, knots):
    steps = len(ahead)
    sublane = lax.broadcasted_iota(jnp.int32, (SUB, LANE), 0)
    table = table_of(coef, 0)
    cells, places, sigma = [], [], []
    before, running = [], None
    for j in range(steps):
        cells.append(buffer[tile, b, pl.ds(j, SUB, stride=steps), :])
        places.append(place_of(cells[j], knots))
        sigma.append(value_at(table, places[j], cells[j]))
        before.append(running)
        running = sigma[j] if running is None else running + sigma[j]
    earlier = running
    for hop in (1, 2, 4):
        earlier = earlier + jnp.where(sublane >= hop, pltpu.roll(earlier, hop, 0), 0.0)
    earlier = earlier - running
    weights = []
    for j in range(steps):
        inside = earlier if j == 0 else earlier + before[j]
        shadow = jnp.exp2(inside * ratio)
        passed = jnp.exp2(sigma[j])
        if ahead[j] is None:
            after = passed
            weights.append((1.0 - passed) * shadow)
        else:
            after = ahead[j] * passed
            weights.append((ahead[j] - after) * shadow)
        ahead[j] = after
    return cells, places, weights


def put_halves(send_ref, keep_ref, sums, tile, bits):
    mine = lax.axis_index("view") & 1
    for q in range(1 << bits - 1):
        octet = 2 * bit_reversed(q, bits - 1)
        for k in range(send_ref.shape[1]):
            send_ref[q, k, tile] = sums[k, pl.ds(octet + 1 - mine, SUB, stride=SUB), :]
            keep_ref[q, k, tile] = sums[k, pl.ds(octet + mine, SUB, stride=SUB), :]


def shade_kernel(
    sigma_scale, ratio, first, total, bits, pieces, far, late, whole_out,
    index_ref, code_ref, tint_ref, tables_ref, density_ref, *rest,
):
    brick_refs = [rest[at * len(pieces) : (at + 1) * len(pieces)] for at in range(far)]
    rest = rest[far * len(pieces) + late :]
    if whole_out:
        out_ref, coef, buffer, lighting, sums, sems = rest
    else:
        send_ref, keep_ref, coef, buffer, lighting, sums, sems = rest
    tiles, layers, slices, _ = buffer.shape
    knots = tables_ref.shape[2]
    steps = slices // SUB
    channels = lighting.shape[0]

    @pl.loop(0, tiles)
    def _(tile):
        fetch_tile(density_ref, buffer, sems, first, tile).start()

    fill_coefficients(index_ref[0, 0], tables_ref, coef, sigma_scale, tables_ref.shape[1])
    fill_lighting(pieces, brick_refs, code_ref, tint_ref, lighting, first, total)

    @pl.loop(0, tiles)
    def _(tile):
        fetch_tile(density_ref, buffer, sems, first, tile).wait()
        columns = pl.ds(pl.multiple_of(tile * LANE, LANE), LANE)
        ahead = [None] * steps
        for b in range(layers):
            cells, places, weights = weights_of(coef, buffer, tile, b, ahead, ratio, knots)
            for k in range(channels):
                lit = jnp.broadcast_to(lighting[k, b : b + 1, columns], (SUB, LANE))
                table = [entry * lit for entry in table_of(coef, k + 1)]
                for j in range(steps):
                    rows = pl.ds(j * SUB, SUB)
                    term = value_at(table, places[j], cells[j]) * weights[j]
                    if b == 0:
                        sums[k, rows] = term
                    else:
                        sums[k, rows] = sums[k, rows] + term
        if whole_out:
            for j in range(steps):
                sums[channels, pl.ds(j * SUB, SUB)] = ahead[j]
            for octet in range(SUB):
                for k in range(channels + 1):
                    for part in range(steps // SUB):
                        out_ref[k, tile, pl.ds(octet * steps + part * SUB, SUB)] = sums[
                            k, pl.ds(part * SUB * SUB + octet, SUB, stride=SUB), :
                        ]
        else:
            put_halves(send_ref, keep_ref, sums, tile, bits)


def unlit_kernel(sigma_scale, ratio, first, late, index_ref, tables_ref, density_ref, *rest):
    out_ref, coef, buffer, sems = rest[late:]
    tiles, layers, slices, _ = buffer.shape
    knots = tables_ref.shape[2]
    steps = slices // SUB

    @pl.loop(0, tiles)
    def _(tile):
        fetch_tile(density_ref, buffer, sems, first, tile).start()

    fill_coefficients(index_ref[0, 0], tables_ref, coef, sigma_scale, tables_ref.shape[1])

    @pl.loop(0, tiles)
    def _(tile):
        fetch_tile(density_ref, buffer, sems, first, tile).wait()
        ahead = [None] * steps
        for b in range(layers):
            cells, places, weights = weights_of(coef, buffer, tile, b, ahead, ratio, knots)
            for k in range(out_ref.shape[2]):
                table = table_of(coef, k + 1)
                for j in range(steps):
                    term = value_at(table, places[j], cells[j]) * weights[j]
                    out_ref[tile, b, k, j * SUB : j * SUB + SUB] = term


def lit_kernel(first, total, bits, pieces, far, late, code_ref, tint_ref, unlit_ref, *rest):
    brick_refs = [rest[at * len(pieces) : (at + 1) * len(pieces)] for at in range(far)]
    send_ref, keep_ref, lighting, sums = rest[far * len(pieces) + late :]
    tiles, layers, channels, slices, _ = unlit_ref.shape
    fill_lighting(pieces, brick_refs, code_ref, tint_ref, lighting, first, total)

    @pl.loop(0, tiles)
    def _(tile):
        columns = pl.ds(pl.multiple_of(tile * LANE, LANE), LANE)
        for k in range(channels):
            lit = [
                jnp.broadcast_to(lighting[k, b : b + 1, columns], (SUB, LANE))
                for b in range(layers)
            ]
            for j in range(slices // SUB):
                rows = slice(j * SUB, j * SUB + SUB)
                terms = [unlit_ref[tile, b, k, rows] * lit[b] for b in range(layers)]
                sums[k, rows] = functools.reduce(jnp.add, terms)
        put_halves(send_ref, keep_ref, sums, tile, bits)


VMEM = functools.partial(pl.BlockSpec, memory_space=pltpu.VMEM)
SMEM = functools.partial(pl.BlockSpec, memory_space=pltpu.SMEM)
ANY = functools.partial(pl.BlockSpec, memory_space=pl.ANY)
HBM = functools.partial(pl.BlockSpec, memory_space=pltpu.HBM)


def shape(*dims):
    return jax.ShapeDtypeStruct(dims, F32)


def cost(density, columns, per_cell):
    cells = density.shape[0] * density.shape[1] * columns
    return pl.CostEstimate(flops=cells * per_cell, bytes_accessed=4 * cells, transcendentals=0)


MERGE_COST = pl.CostEstimate(flops=2 * 10**10, bytes_accessed=2**20, transcendentals=0)


def sums(density, tables, index, low, high, sigma_scale, ratio, bits, split):
    layers, slices, _ = density.shape
    tiles = (high - low) // LANE
    half = (1 << bits) // 2
    outs = [shape(layers, high - low)]
    scratch = [pltpu.VMEM((4, SUB, LANE), F32), pltpu.VMEM((tiles, layers, slices, LANE), F32)]
    if split:
        outs += [shape(half, tiles, SUB, LANE)] * 2
        scratch.append(pltpu.VMEM((slices // SUB, SUB, LANE), F32))
    scratch.append(pltpu.SemaphoreType.DMA((tiles,)))
    return pl.pallas_call(
        functools.partial(sums_kernel, sigma_scale, ratio, low, bits, split),
        in_specs=[SMEM(), VMEM(), HBM()],
        out_specs=[VMEM()] * len(outs),
        out_shape=outs,
        scratch_shapes=scratch,
        compiler_params=params(STREAM_LIMIT),
        cost_estimate=cost(density, high - low, 4000),
        name="sums",
    )(index, tables, density)


def shade(
    density, tables, index, code, tint, bricks, pieces, low, high, sigma_scale, ratio, bits,
    whole_out, after=(),
):
    layers, slices, total = density.shape
    channels = tint.shape[1]
    tiles = (high - low) // LANE
    half = (1 << bits) // 2
    if whole_out:
        outs = [shape(channels + 1, tiles, slices, LANE)]
    else:
        outs = [shape(half, channels, tiles, SUB, LANE)] * 2
    operands = [row for rows in bricks for row in rows]
    return pl.pallas_call(
        functools.partial(
            shade_kernel, sigma_scale, ratio, low, total, bits, pieces, len(bricks), len(after),
            whole_out,
        ),
        in_specs=[SMEM()] * 3 + [VMEM(), HBM()] + [VMEM()] * len(operands) + [ANY()] * len(after),
        out_specs=[VMEM()] * len(outs),
        out_shape=outs,
        scratch_shapes=[
            pltpu.VMEM((4 * tables.shape[1], SUB, LANE), F32),
            pltpu.VMEM((tiles, layers, slices, LANE), F32),
            pltpu.VMEM((channels, layers, high - low), F32),
            pltpu.VMEM((channels + 1, slices, LANE), F32),
            pltpu.SemaphoreType.DMA((tiles,)),
        ],
        compiler_params=params(),
        cost_estimate=cost(density, high - low, 10000),
        name="shade",
    )(index, code, tint, tables, density, *operands, *after)


def unlit(density, tables, index, low, high, sigma_scale, ratio, after=()):
    layers, slices, _ = density.shape
    tiles = (high - low) // LANE
    return pl.pallas_call(
        functools.partial(unlit_kernel, sigma_scale, ratio, low, len(after)),
        in_specs=[SMEM(), VMEM(), HBM()] + [ANY()] * len(after),
        out_specs=VMEM(),
        out_shape=shape(tiles, layers, tables.shape[1] - 1, slices, LANE),
        scratch_shapes=[
            pltpu.VMEM((4 * tables.shape[1], SUB, LANE), F32),
            pltpu.VMEM((tiles, layers, slices, LANE), F32),
            pltpu.SemaphoreType.DMA((tiles,)),
        ],
        compiler_params=params(),
        cost_estimate=cost(density, high - low, 10000),
        name="unlit",
    )(index, tables, density, *after)


def lit(cells, code, tint, bricks, pieces, low, high, total, bits, after=()):
    tiles, layers, channels, slices, _ = cells.shape
    half = (1 << bits) // 2
    operands = [row for rows in bricks for row in rows]
    return pl.pallas_call(
        functools.partial(
            lit_kernel, low, total, bits, pieces, len(bricks), len(after)
        ),
        in_specs=[SMEM()] * 2 + [VMEM()] * (1 + len(operands)) + [ANY()] * len(after),
        out_specs=[VMEM()] * 2,
        out_shape=[shape(half, channels, tiles, SUB, LANE)] * 2,
        scratch_shapes=[
            pltpu.VMEM((channels, layers, high - low), F32),
            pltpu.VMEM((channels, slices, LANE), F32),
        ],
        compiler_params=params(),
        name="lit",
    )(code, tint, cells, *operands, *after)


def merge_clear_kernel(bit, own_ref, other_ref, *rest):
    send_ref, keep_ref = rest[-2:]
    half = send_ref.shape[0]
    mine = lax.axis_index("view") >> bit + 1 & 1
    for at in range(half):
        there, here = (1 - mine) * half + at, mine * half + at
        send_ref[at] = own_ref[there] * other_ref[there]
        keep_ref[at] = own_ref[here] * other_ref[here]


def merge_clear(own, other, bit, after=()):
    half = shape(own.shape[0] // 2, *own.shape[1:])
    return pl.pallas_call(
        functools.partial(merge_clear_kernel, bit),
        in_specs=[VMEM()] * 2 + [ANY()] * len(after),
        out_specs=[VMEM()] * 2,
        out_shape=[half] * 2,
        compiler_params=params(),
        cost_estimate=MERGE_COST,
        name="merge_clear",
    )(own, other, *after)


def merge_kernel(bit, start, own_ref, other_ref, own_clear_ref, other_clear_ref, *rest):
    send_ref, keep_ref = rest[-2:]
    tiles = pl.ds(start, own_ref.shape[2])
    half = send_ref.shape[0]
    me = lax.axis_index("view")
    mine = me >> bit + 1 & 1

    def merged(front_ref, back_ref, clear_ref):
        for at in range(half):
            for to_ref, side in ((send_ref, 1 - mine), (keep_ref, mine)):
                source = side * half + at
                clear = clear_ref[source, tiles]
                for k in range(send_ref.shape[1]):
                    to_ref[at, k] = front_ref[source, k] + clear * back_ref[source, k]

    upper = me >> bit & 1 == 1

    @pl.when(upper)
    def _():
        merged(other_ref, own_ref, other_clear_ref)

    @pl.when(jnp.logical_not(upper))
    def _():
        merged(own_ref, other_ref, own_clear_ref)


def merge(own, other, own_clear, other_clear, bit, low, after=()):
    half = shape(own.shape[0] // 2, *own.shape[1:])
    return pl.pallas_call(
        functools.partial(merge_kernel, bit, low // LANE),
        in_specs=[VMEM()] * 4 + [ANY()] * len(after),
        out_specs=[VMEM()] * 2,
        out_shape=[half] * 2,
        compiler_params=params(),
        cost_estimate=MERGE_COST,
        name="merge",
    )(own, other, own_clear, other_clear, *after)


def last_kernel(bit, firsts, *refs):
    chunks = len(firsts)
    own_clear_ref, other_clear_ref = refs[2 * chunks : 2 * chunks + 2]
    image_ref = refs[-1]
    upper = lax.axis_index("view") >> bit & 1 == 1

    def merged(fronts, backs, clear_ref):
        for first, front_ref, back_ref in zip(firsts, fronts, backs):
            channels, tiles = front_ref.shape[1:3]
            for tile in range(tiles):
                columns = slice(first + tile * LANE, first + tile * LANE + LANE)
                clear = clear_ref[0, first // LANE + tile]
                for k in range(channels):
                    image_ref[k, :, columns] = front_ref[0, k, tile] + clear * back_ref[0, k, tile]

    for tile in range(own_clear_ref.shape[1]):
        columns = slice(tile * LANE, tile * LANE + LANE)
        image_ref[image_ref.shape[0] - 1, :, columns] = own_clear_ref[0, tile] * other_clear_ref[0, tile]

    @pl.when(upper)
    def _():
        merged(refs[chunks : 2 * chunks], refs[:chunks], other_clear_ref)

    @pl.when(jnp.logical_not(upper))
    def _():
        merged(refs[:chunks], refs[chunks : 2 * chunks], own_clear_ref)


def last(owns, others, own_clear, other_clear, bit, firsts, total):
    return pl.pallas_call(
        functools.partial(last_kernel, bit, firsts),
        in_specs=[VMEM()] * (2 * len(owns) + 2),
        out_specs=VMEM(),
        out_shape=shape(owns[0].shape[1] + 1, SUB, total),
        compiler_params=params(),
        name="last",
    )(*owns, *others, own_clear, other_clear)


def swap(block, bit):
    count = lax.axis_size("view")
    return lax.ppermute(block, "view", [(at, at ^ 1 << bit) for at in range(count)])


def from_earlier(leaving):
    count = lax.axis_size("light")
    return [
        lax.ppermute(leaving, "light", [(at, at + apart) for at in range(count - apart)])
        for apart in range(1, count)
    ]


def composite_over(front, back):
    clear = front[-1:]
    return jnp.concatenate([front[:-1] + clear * back[:-1], clear * back[-1:]])


def plain(density, tables, table_index, light_code, light_tint, sigma_scale, ratio, bits):
    slices, total = density.shape[1:]
    [leaving] = sums(density, tables, table_index, 0, total, sigma_scale, ratio, 0, False)
    bricks = [[row] for row in from_earlier(leaving)]
    parts = shade(
        density, tables, table_index, light_code, light_tint, bricks, [(0, total)], 0, total,
        sigma_scale, ratio, 0, True,
    )[0]
    rows = slices >> bits
    depth = parts.shape[0]
    current = parts.transpose(0, 2, 1, 3).reshape((depth,) + (2,) * bits + (rows, total))
    current = current.transpose((0,) + tuple(range(bits, 0, -1)) + (bits + 1, bits + 2))
    for bit in range(bits):
        upper = lax.axis_index("view") >> bit & 1 == 1
        first, second = current[:, 0], current[:, 1]
        kept = jnp.where(upper, second, first)
        arrived = swap(jnp.where(upper, first, second), bit)
        current = composite_over(jnp.where(upper, arrived, kept), jnp.where(upper, kept, arrived))
    return current.reshape(depth, rows, total)


CUTS = (0.25, 0.625)


def ranges(cuts, total):
    ends = [0] + [round(total * cut / LANE) * LANE for cut in cuts] + [total]
    return list(zip(ends[:-1], ends[1:]))


def local(density, tables, table_index, light_code, light_tint):
    layers, slices, total = density.shape
    views = lax.axis_size("view")
    bits = views.bit_length() - 1
    sigma_scale = -math.log2(math.e) / (layers * views)
    ratio = layers * views / (slices * lax.axis_size("light"))
    if views * SUB != slices or bits != 3:
        return plain(
            density, tables, table_index, light_code, light_tint, sigma_scale, ratio, bits
        )
    pieces = [(0, total)]
    chunks = ranges(CUTS, total)
    leaving, send, keep = sums(
        density, tables, table_index, 0, total, sigma_scale, ratio, bits, True
    )
    bricks = [[row] for row in from_earlier(leaving)]
    clear = [(keep, swap(send, 0))]
    send, keep = merge_clear(*clear[0], 0)
    clear.append((keep, swap(send, 1)))
    first = unlit(
        density, tables, table_index, *chunks[0], sigma_scale, ratio, after=(send,)
    )
    state = [None] * len(chunks)
    state[0] = lit(first, light_code, light_tint, bricks, pieces, *chunks[0], total, bits)
    send, keep = merge_clear(*clear[1], 1, after=(state[0][0],))
    clear.append((keep, swap(send, 2)))
    done = send
    for at, (low, high) in enumerate(chunks):
        if at:
            state[at] = shade(
                density, tables, table_index, light_code, light_tint, bricks, pieces, low, high,
                sigma_scale, ratio, bits, False, after=(done,),
            )
            done = state[at][0]
        send, keep = state[at]
        arrived = swap(send, 0)
        if at:
            before = chunks[at - 1][0]
            settled = state[at - 2][1] if at > 1 else clear[2][1]
            late = merge(*state[at - 1], *clear[1], 1, before, after=(done, settled))
            state[at - 1] = (late[1], swap(late[0], 2))
            done = late[0]
        send, keep = merge(keep, arrived, *clear[0], 0, low, after=(done,))
        done = send
        state[at] = (keep, swap(send, 1))
    late = merge(*state[-1], *clear[1], 1, chunks[-1][0], after=(state[-2][1],))
    state[-1] = (late[1], swap(late[0], 2))
    owns, others = zip(*state)
    return last(owns, others, *clear[2], 2, [low for low, _ in chunks], total)


def solution(mesh):
    return jax.shard_map(
        local,
        mesh=mesh,
        in_specs=(P("view", "light", None), P(), P("light", "view"), P(), P()),
        out_specs=P(None, ("light", "view"), None),
        check_vma=False,
    )
```

```python
import functools
import math

import jax
import jax.numpy as jnp
from jax import lax
from jax.experimental import pallas as pl
from jax.experimental.pallas import tpu as pltpu
from jax.sharding import PartitionSpec as P

LANE = 128
SUB = 8
DRIFTS = (-1, 0, 1)
VMEM_LIMIT = 24 * 2**20
STREAM_LIMIT = 44 * 2**20
F32 = jnp.float32


def params(limit=VMEM_LIMIT):
    return pltpu.CompilerParams(vmem_limit_bytes=limit)


def bit_reversed(value, bits):
    return sum((value >> at & 1) << bits - 1 - at for at in range(bits))


def rows_of(table, index):
    return jnp.take_along_axis(table, index, axis=0, mode="promise_in_bounds")


def fill_coefficients(table_ref, coef, sigma_scale):
    rows = table_ref[...]
    knots = rows.shape[1]
    at_row = lax.broadcasted_iota(jnp.int32, (2 * SUB, knots), 0)
    at_col = lax.broadcasted_iota(jnp.int32, (2 * SUB, knots), 1)
    left_at = jnp.minimum(at_row, knots - 2)
    for q in range(rows.shape[0]):
        row = jnp.broadcast_to(rows[q : q + 1], (2 * SUB, knots))
        left = jnp.sum(jnp.where(at_col == left_at, row, 0.0), axis=1, keepdims=True)
        right = jnp.sum(jnp.where(at_col == left_at + 1, row, 0.0), axis=1, keepdims=True)
        step = right - left
        start = left - step * left_at[:, :1].astype(F32)
        scale = sigma_scale if q == 0 else 1.0
        start = jnp.broadcast_to(start * scale, (2 * SUB, LANE))
        step = jnp.broadcast_to(step * (scale * (knots - 1)), (2 * SUB, LANE))
        coef[4 * q] = start[:SUB]
        coef[4 * q + 1] = start[SUB:]
        coef[4 * q + 2] = step[:SUB]
        coef[4 * q + 3] = step[SUB:]


def place_of(cells, knots):
    knot = (cells * (knots - 1.0)).astype(jnp.int32)
    return knot & (SUB - 1), knot >= SUB


def value_at(table, place, cells):
    low, high = place
    start = jnp.where(high, rows_of(table[1], low), rows_of(table[0], low))
    step = jnp.where(high, rows_of(table[3], low), rows_of(table[2], low))
    return start + step * cells


def table_of(coef, q):
    return [coef[4 * q + at] for at in range(4)]


def fetch_tile(density_ref, cells_ref, sems, tile):
    columns = pl.ds(pl.multiple_of(tile * LANE, LANE), LANE)
    return pltpu.make_async_copy(density_ref.at[:, :, columns], cells_ref.at[tile], sems.at[tile])


def sums_kernel(sigma_scale, ratio, bits, split, table_ref, density_ref, *rest):
    if split:
        leaving_ref, cells_ref, coef, send_ref, keep_ref, clear, sems = rest
    else:
        leaving_ref, cells_ref, coef, sems = rest
    tiles, layers, slices, _ = cells_ref.shape
    knots = table_ref.shape[1]

    @pl.loop(0, tiles)
    def _(tile):
        fetch_tile(density_ref, cells_ref, sems, tile).start()

    fill_coefficients(table_ref, coef, sigma_scale)
    mine = lax.axis_index("view") & 1 if split else 0
    half = (1 << bits) // 2

    @pl.loop(0, tiles)
    def _(tile):
        fetch_tile(density_ref, cells_ref, sems, tile).wait()
        table = table_of(coef, 0)
        down = [jnp.zeros((SUB, LANE), F32) for _ in range(layers)]
        for block in range(slices // SUB):
            through = jnp.zeros((SUB, LANE), F32)
            for b in range(layers):
                cells = cells_ref[tile, b, block * SUB : block * SUB + SUB]
                sigma = value_at(table, place_of(cells, knots), cells)
                through = through + sigma
                down[b] = down[b] + sigma
            if split:
                clear[block] = jnp.exp2(through)
        columns = pl.ds(pl.multiple_of(tile * LANE, LANE), LANE)
        for b in range(layers):
            leaving_ref[b : b + 1, columns] = jnp.exp2(
                jnp.sum(down[b], axis=0, keepdims=True) * ratio
            )
        if split:
            for q in range(half):
                octet = 2 * bit_reversed(q, bits - 1)
                send_ref[q, tile] = clear[octet + 1 - mine]
                keep_ref[q, tile] = clear[octet + mine]


def fill_lighting(pieces, brick_refs, code_ref, tint_ref, lighting, first, total):
    layers, width = lighting.shape[1:]
    wide = width + 2 * LANE
    place = lax.broadcasted_iota(jnp.int32, (layers, wide), 1) + (first - LANE)
    inside = jnp.logical_and(place >= 0, place < total).astype(F32)
    mine = lax.axis_index("light")
    fronts = [inside] * len(DRIFTS)
    for apart in range(len(brick_refs), 0, -1):
        parts, at = [], first - LANE
        if at < 0:
            parts.append(jnp.zeros((layers, -at), F32))
            at = 0
        for (low, high), ref in zip(pieces, brick_refs[apart - 1]):
            stop = min(high, first + width + LANE)
            if at < stop and at >= low:
                parts.append(ref[:, at - low : stop - low])
                at = stop
        if at < first + width + LANE:
            parts.append(jnp.zeros((layers, first + width + LANE - at), F32))
        leaving = jnp.concatenate(parts, axis=1)
        active = mine >= apart
        result = []
        shared = None
        for drift, front in zip(DRIFTS, fronts):
            if shared is None or apart < len(brick_refs):
                row = front * leaving
                shared = 0.5 * row + 0.25 * (pltpu.roll(row, 1, 1) + pltpu.roll(row, wide - 1, 1))
            moved = shared if drift == 0 else pltpu.roll(shared, drift % wide, 1)
            result.append(jnp.where(active, moved * inside, front))
        fronts = result
    for k in range(lighting.shape[0]):
        shade = jnp.zeros((layers, wide), F32)
        for drift, front in zip(DRIFTS, fronts):
            tint = 0.0
            for light in range(tint_ref.shape[0]):
                tint = tint + jnp.where(code_ref[light] == drift, tint_ref[light, k], 0.0)
            shade = shade + tint * front
        lighting[k] = shade[:, LANE : LANE + width]


def weights_of(coef, cells_ref, tile, b, ahead, ratio, knots):
    steps = len(ahead)
    sublane = lax.broadcasted_iota(jnp.int32, (SUB, LANE), 0)
    table = table_of(coef, 0)
    cells, places, sigma = [], [], []
    before, running = [], None
    for j in range(steps):
        cells.append(cells_ref[tile, b, pl.ds(j, SUB, stride=steps), :])
        places.append(place_of(cells[j], knots))
        sigma.append(value_at(table, places[j], cells[j]))
        before.append(running)
        running = sigma[j] if running is None else running + sigma[j]
    earlier = running
    for hop in (1, 2, 4):
        earlier = earlier + jnp.where(sublane >= hop, pltpu.roll(earlier, hop, 0), 0.0)
    earlier = earlier - running
    weights = []
    for j in range(steps):
        inside = earlier if j == 0 else earlier + before[j]
        shadow = jnp.exp2(inside * ratio)
        passed = jnp.exp2(sigma[j])
        if ahead[j] is None:
            after = passed
            weights.append((1.0 - passed) * shadow)
        else:
            after = ahead[j] * passed
            weights.append((ahead[j] - after) * shadow)
        ahead[j] = after
    return cells, places, weights


def put_halves(send_ref, keep_ref, sums, tile, bits):
    mine = lax.axis_index("view") & 1
    for q in range(1 << bits - 1):
        octet = 2 * bit_reversed(q, bits - 1)
        for k in range(send_ref.shape[1]):
            send_ref[q, k, tile] = sums[k, pl.ds(octet + 1 - mine, SUB, stride=SUB), :]
            keep_ref[q, k, tile] = sums[k, pl.ds(octet + mine, SUB, stride=SUB), :]


def shade_kernel(
    ratio, knots, first, total, bits, pieces, far, late, whole_out,
    code_ref, tint_ref, coef, cells_ref, *rest,
):
    brick_refs = [rest[at * len(pieces) : (at + 1) * len(pieces)] for at in range(far)]
    rest = rest[far * len(pieces) + late :]
    if whole_out:
        out_ref, lighting, sums = rest
    else:
        send_ref, keep_ref, lighting, sums = rest
    layers, slices = cells_ref.shape[1:3]
    steps = slices // SUB
    channels = lighting.shape[0]
    fill_lighting(pieces, brick_refs, code_ref, tint_ref, lighting, first, total)

    @pl.loop(0, lighting.shape[2] // LANE)
    def _(tile):
        columns = pl.ds(pl.multiple_of(tile * LANE, LANE), LANE)
        ahead = [None] * steps
        for b in range(layers):
            cells, places, weights = weights_of(
                coef, cells_ref, first // LANE + tile, b, ahead, ratio, knots
            )
            for k in range(channels):
                lit = jnp.broadcast_to(lighting[k, b : b + 1, columns], (SUB, LANE))
                table = [entry * lit for entry in table_of(coef, k + 1)]
                for j in range(steps):
                    rows = pl.ds(j * SUB, SUB)
                    term = value_at(table, places[j], cells[j]) * weights[j]
                    if b == 0:
                        sums[k, rows] = term
                    else:
                        sums[k, rows] = sums[k, rows] + term
        if whole_out:
            for j in range(steps):
                sums[channels, pl.ds(j * SUB, SUB)] = ahead[j]
            for octet in range(SUB):
                for k in range(channels + 1):
                    for part in range(steps // SUB):
                        out_ref[k, tile, pl.ds(octet * steps + part * SUB, SUB)] = sums[
                            k, pl.ds(part * SUB * SUB + octet, SUB, stride=SUB), :
                        ]
        else:
            put_halves(send_ref, keep_ref, sums, tile, bits)


def unlit_kernel(ratio, knots, first, late, coef, cells_ref, *rest):
    out_ref = rest[late]
    tiles, layers, channels, slices, _ = out_ref.shape
    steps = slices // SUB

    @pl.loop(0, tiles)
    def _(tile):
        ahead = [None] * steps
        for b in range(layers):
            cells, places, weights = weights_of(
                coef, cells_ref, first // LANE + tile, b, ahead, ratio, knots
            )
            for k in range(channels):
                table = table_of(coef, k + 1)
                for j in range(steps):
                    term = value_at(table, places[j], cells[j]) * weights[j]
                    out_ref[tile, b, k, j * SUB : j * SUB + SUB] = term


def lit_kernel(first, total, bits, pieces, far, late, code_ref, tint_ref, unlit_ref, *rest):
    brick_refs = [rest[at * len(pieces) : (at + 1) * len(pieces)] for at in range(far)]
    send_ref, keep_ref, lighting, sums = rest[far * len(pieces) + late :]
    tiles, layers, channels, slices, _ = unlit_ref.shape
    fill_lighting(pieces, brick_refs, code_ref, tint_ref, lighting, first, total)

    @pl.loop(0, tiles)
    def _(tile):
        columns = pl.ds(pl.multiple_of(tile * LANE, LANE), LANE)
        for k in range(channels):
            lit = [
                jnp.broadcast_to(lighting[k, b : b + 1, columns], (SUB, LANE))
                for b in range(layers)
            ]
            for j in range(slices // SUB):
                rows = slice(j * SUB, j * SUB + SUB)
                terms = [unlit_ref[tile, b, k, rows] * lit[b] for b in range(layers)]
                sums[k, rows] = functools.reduce(jnp.add, terms)
        put_halves(send_ref, keep_ref, sums, tile, bits)


VMEM = functools.partial(pl.BlockSpec, memory_space=pltpu.VMEM)
SMEM = functools.partial(pl.BlockSpec, memory_space=pltpu.SMEM)
ANY = functools.partial(pl.BlockSpec, memory_space=pl.ANY)
HBM = functools.partial(pl.BlockSpec, memory_space=pltpu.HBM)


def shape(*dims):
    return jax.ShapeDtypeStruct(dims, F32)


def cost(cells, columns, per_cell):
    count = cells.shape[1] * cells.shape[2] * columns
    return pl.CostEstimate(flops=count * per_cell, bytes_accessed=4 * count, transcendentals=0)


MERGE_COST = pl.CostEstimate(flops=2 * 10**10, bytes_accessed=2**20, transcendentals=0)


def sums(density, table, sigma_scale, ratio, bits, split):
    layers, slices, total = density.shape
    tiles = total // LANE
    half = (1 << bits) // 2
    outs = [
        shape(layers, total),
        shape(tiles, layers, slices, LANE),
        shape(4 * table.shape[0], SUB, LANE),
    ]
    cells_shape = outs[1]
    scratch = []
    if split:
        outs += [shape(half, tiles, SUB, LANE)] * 2
        scratch.append(pltpu.VMEM((slices // SUB, SUB, LANE), F32))
    scratch.append(pltpu.SemaphoreType.DMA((tiles,)))
    return pl.pallas_call(
        functools.partial(sums_kernel, sigma_scale, ratio, bits, split),
        in_specs=[VMEM(), HBM()],
        out_specs=[VMEM()] * len(outs),
        out_shape=outs,
        scratch_shapes=scratch,
        compiler_params=params(STREAM_LIMIT),
        cost_estimate=cost(cells_shape, total, 4000),
        name="sums",
    )(table, density)


def shade(coef, cells, knots, code, tint, bricks, pieces, low, high, ratio, bits, whole_out, after=()):
    tiles, layers, slices, _ = cells.shape
    channels = tint.shape[1]
    half = (1 << bits) // 2
    if whole_out:
        outs = [shape(channels + 1, (high - low) // LANE, slices, LANE)]
    else:
        outs = [shape(half, channels, (high - low) // LANE, SUB, LANE)] * 2
    operands = [row for rows in bricks for row in rows]
    return pl.pallas_call(
        functools.partial(
            shade_kernel, ratio, knots, low, tiles * LANE, bits, pieces, len(bricks), len(after),
            whole_out,
        ),
        in_specs=[SMEM()] * 2 + [VMEM()] * (2 + len(operands)) + [ANY()] * len(after),
        out_specs=[VMEM()] * len(outs),
        out_shape=outs,
        scratch_shapes=[
            pltpu.VMEM((channels, layers, high - low), F32),
            pltpu.VMEM((channels + 1, slices, LANE), F32),
        ],
        compiler_params=params(),
        cost_estimate=cost(cells, high - low, 10000),
        name="shade",
    )(code, tint, coef, cells, *operands, *after)


def unlit(coef, cells, knots, channels, low, high, ratio, after=()):
    layers, slices = cells.shape[1:3]
    return pl.pallas_call(
        functools.partial(unlit_kernel, ratio, knots, low, len(after)),
        in_specs=[VMEM()] * 2 + [ANY()] * len(after),
        out_specs=VMEM(),
        out_shape=shape((high - low) // LANE, layers, channels, slices, LANE),
        compiler_params=params(),
        cost_estimate=cost(cells, high - low, 10000),
        name="unlit",
    )(coef, cells, *after)


def lit(cells, code, tint, bricks, pieces, low, high, total, bits, after=()):
    tiles, layers, channels, slices, _ = cells.shape
    half = (1 << bits) // 2
    operands = [row for rows in bricks for row in rows]
    return pl.pallas_call(
        functools.partial(
            lit_kernel, low, total, bits, pieces, len(bricks), len(after)
        ),
        in_specs=[SMEM()] * 2 + [VMEM()] * (1 + len(operands)) + [ANY()] * len(after),
        out_specs=[VMEM()] * 2,
        out_shape=[shape(half, channels, tiles, SUB, LANE)] * 2,
        scratch_shapes=[
            pltpu.VMEM((channels, layers, high - low), F32),
            pltpu.VMEM((channels, slices, LANE), F32),
        ],
        compiler_params=params(),
        name="lit",
    )(code, tint, cells, *operands, *after)


def merge_clear_kernel(bit, own_ref, other_ref, *rest):
    send_ref, keep_ref = rest[-2:]
    half = send_ref.shape[0]
    mine = lax.axis_index("view") >> bit + 1 & 1
    for at in range(half):
        there, here = (1 - mine) * half + at, mine * half + at
        send_ref[at] = own_ref[there] * other_ref[there]
        keep_ref[at] = own_ref[here] * other_ref[here]


def merge_clear(own, other, bit, after=()):
    half = shape(own.shape[0] // 2, *own.shape[1:])
    return pl.pallas_call(
        functools.partial(merge_clear_kernel, bit),
        in_specs=[VMEM()] * 2 + [ANY()] * len(after),
        out_specs=[VMEM()] * 2,
        out_shape=[half] * 2,
        compiler_params=params(),
        cost_estimate=MERGE_COST,
        name="merge_clear",
    )(own, other, *after)


def merge_kernel(bit, start, joined, own_ref, other_ref, own_clear_ref, other_clear_ref, *rest):
    send_ref, keep_ref = rest[-2:]
    half, channels, count = keep_ref.shape[:3]
    tiles = pl.ds(start, count)
    me = lax.axis_index("view")
    mine = me >> bit + 1 & 1

    def merged(front_ref, back_ref, clear_ref):
        for at in range(half):
            for to_ref, side in ((send_ref, 1 - mine), (keep_ref, mine)):
                source = side * half + at
                clear = clear_ref[source, tiles]
                for k in range(channels):
                    value = front_ref[source, k] + clear * back_ref[source, k]
                    if joined and to_ref is send_ref:
                        send_ref[k * count : (k + 1) * count] = value
                    else:
                        to_ref[at, k] = value

    upper = me >> bit & 1 == 1

    @pl.when(upper)
    def _():
        merged(other_ref, own_ref, other_clear_ref)

    @pl.when(jnp.logical_not(upper))
    def _():
        merged(own_ref, other_ref, own_clear_ref)

    if joined:
        send_ref[channels * count :] = rest[0][0]


def merge(own, other, own_clear, other_clear, bit, low, joined=(), after=()):
    count, channels, tiles = own.shape[:3]
    half = shape(count // 2, *own.shape[1:])
    outs = [half] * 2
    if joined:
        outs = [shape(channels * tiles + joined[0].shape[1], SUB, LANE), half]
    return pl.pallas_call(
        functools.partial(merge_kernel, bit, low // LANE, bool(joined)),
        in_specs=[VMEM()] * (4 + len(joined)) + [ANY()] * len(after),
        out_specs=[VMEM()] * len(outs),
        out_shape=outs,
        compiler_params=params(),
        cost_estimate=MERGE_COST,
        name="merge",
    )(own, other, own_clear, other_clear, *joined, *after)


def last_kernel(bit, firsts, *refs):
    chunks = len(firsts)
    owns, others = refs[:chunks], refs[chunks : 2 * chunks]
    own_clear_ref, image_ref = refs[2 * chunks :]
    channels, joined_tiles = owns[0].shape[1:3]
    upper = lax.axis_index("view") >> bit & 1 == 1

    def other_clear(tile):
        return others[0][channels * joined_tiles + tile]

    def merged(swapped):
        for at, first in enumerate(firsts):
            for tile in range(owns[at].shape[2]):
                columns = slice(first + tile * LANE, first + tile * LANE + LANE)
                whole = first // LANE + tile
                clear = other_clear(whole) if swapped else own_clear_ref[0, whole]
                for k in range(channels):
                    own = owns[at][0, k, tile]
                    other = others[at][k * joined_tiles + tile] if at == 0 else others[at][0, k, tile]
                    front, back = (other, own) if swapped else (own, other)
                    image_ref[k, :, columns] = front + clear * back

    for tile in range(own_clear_ref.shape[1]):
        columns = slice(tile * LANE, tile * LANE + LANE)
        image_ref[channels, :, columns] = own_clear_ref[0, tile] * other_clear(tile)

    @pl.when(upper)
    def _():
        merged(True)

    @pl.when(jnp.logical_not(upper))
    def _():
        merged(False)


def last(owns, others, own_clear, bit, firsts, total):
    return pl.pallas_call(
        functools.partial(last_kernel, bit, firsts),
        in_specs=[VMEM()] * (2 * len(owns) + 1),
        out_specs=VMEM(),
        out_shape=shape(owns[0].shape[1] + 1, SUB, total),
        compiler_params=params(),
        name="last",
    )(*owns, *others, own_clear)


def swap(block, bit):
    count = lax.axis_size("view")
    return lax.ppermute(block, "view", [(at, at ^ 1 << bit) for at in range(count)])


def from_earlier(leaving):
    count = lax.axis_size("light")
    return [
        lax.ppermute(leaving, "light", [(at, at + apart) for at in range(count - apart)])
        for apart in range(1, count)
    ]


def composite_over(front, back):
    clear = front[-1:]
    return jnp.concatenate([front[:-1] + clear * back[:-1], clear * back[-1:]])


def plain(density, table, light_code, light_tint, sigma_scale, ratio, bits):
    slices, total = density.shape[1:]
    leaving, cells, coef = sums(density, table, sigma_scale, ratio, 0, False)
    bricks = [[row] for row in from_earlier(leaving)]
    parts = shade(
        coef, cells, table.shape[1], light_code, light_tint, bricks, [(0, total)], 0, total, ratio,
        0, True,
    )[0]
    rows = slices >> bits
    depth = parts.shape[0]
    current = parts.transpose(0, 2, 1, 3).reshape((depth,) + (2,) * bits + (rows, total))
    current = current.transpose((0,) + tuple(range(bits, 0, -1)) + (bits + 1, bits + 2))
    for bit in range(bits):
        upper = lax.axis_index("view") >> bit & 1 == 1
        first, second = current[:, 0], current[:, 1]
        kept = jnp.where(upper, second, first)
        arrived = swap(jnp.where(upper, first, second), bit)
        current = composite_over(jnp.where(upper, arrived, kept), jnp.where(upper, kept, arrived))
    return current.reshape(depth, rows, total)


CUTS = (0.25, 0.6875)


def ranges(cuts, total):
    ends = [0] + [round(total * cut / LANE) * LANE for cut in cuts] + [total]
    return list(zip(ends[:-1], ends[1:]))


def local(density, tables, table_index, light_code, light_tint):
    layers, slices, total = density.shape
    views = lax.axis_size("view")
    bits = views.bit_length() - 1
    sigma_scale = -math.log2(math.e) / (layers * views)
    ratio = layers * views / (slices * lax.axis_size("light"))
    chosen = jnp.arange(tables.shape[0], dtype=jnp.int32) == table_index[0, 0]
    table = jnp.sum(jnp.where(chosen[:, None, None], tables, 0.0), axis=0)
    if views * SUB != slices or bits != 3:
        return plain(density, table, light_code, light_tint, sigma_scale, ratio, bits)
    pieces = [(0, total)]
    chunks = ranges(CUTS, total)
    knots = table.shape[1]
    leaving, cells, coef, send, keep = sums(
        density, table, sigma_scale, ratio, bits, True
    )
    bricks = [[row] for row in from_earlier(leaving)]
    clear = [(keep, swap(send, 0))]
    send, keep = merge_clear(*clear[0], 0)
    clear.append((keep, swap(send, 1)))
    first = unlit(coef, cells, knots, light_tint.shape[1], *chunks[0], ratio, after=(send,))
    state = [lit(first, light_code, light_tint, bricks, pieces, *chunks[0], total, bits)]
    clear_send, own_clear = merge_clear(*clear[1], 1, after=(state[0][0],))
    done = clear_send
    for at, (low, high) in enumerate(chunks):
        if at:
            state.append(
                shade(
                    coef, cells, knots, light_code, light_tint, bricks, pieces, low, high, ratio,
                    bits, False, after=(done,),
                )
            )
            done = state[at][0]
        send, keep = state[at]
        arrived = swap(send, 0)
        if at:
            settled = (done,) if at == 1 else (done, state[at - 2][1])
            late = merge(
                *state[at - 1], *clear[1], 1, chunks[at - 1][0],
                joined=(clear_send,) if at == 1 else (), after=settled,
            )
            state[at - 1] = (late[1], swap(late[0], 2))
            done = late[0]
        send, keep = merge(keep, arrived, *clear[0], 0, low, after=(done,))
        done = send
        state[at] = (keep, swap(send, 1))
    late = merge(*state[-1], *clear[1], 1, chunks[-1][0], after=(state[-2][1],))
    state[-1] = (late[1], swap(late[0], 2))
    owns, others = zip(*state)
    return last(owns, others, own_clear, 2, [low for low, _ in chunks], total)


def solution(mesh):
    return jax.shard_map(
        local,
        mesh=mesh,
        in_specs=(P("view", "light", None), P(), P("light", "view"), P(), P()),
        out_specs=P(None, ("light", "view"), None),
        check_vma=False,
    )
```

```python
import functools

import jax
import jax.numpy as jnp
import numpy as np
from jax import lax
from jax.experimental import pallas as pl
from jax.experimental.pallas import tpu as pltpu
from jax.sharding import PartitionSpec as P

LANE = 128
SUB = 8
DRIFTS = (-1, 0, 1)
VMEM_LIMIT = 16 * 2**20
STREAM_LIMIT = 36 * 2**20
F32 = jnp.float32


def params(limit=VMEM_LIMIT):
    return pltpu.CompilerParams(vmem_limit_bytes=limit)


def bit_reversed(value, bits):
    return sum((value >> at & 1) << bits - 1 - at for at in range(bits))


def rows_of(table, index):
    return jnp.take_along_axis(table, index, axis=0, mode="promise_in_bounds")


def fill_coefficients(table_ref, coef, sigma_scale):
    rows = table_ref[...]
    knots = rows.shape[1]
    at_row = lax.broadcasted_iota(jnp.int32, (2 * SUB, knots), 0)
    at_col = lax.broadcasted_iota(jnp.int32, (2 * SUB, knots), 1)
    left_at = jnp.minimum(at_row, knots - 2)
    for q in range(rows.shape[0]):
        row = jnp.broadcast_to(rows[q : q + 1], (2 * SUB, knots))
        left = jnp.sum(jnp.where(at_col == left_at, row, 0.0), axis=1, keepdims=True)
        right = jnp.sum(jnp.where(at_col == left_at + 1, row, 0.0), axis=1, keepdims=True)
        step = right - left
        start = left - step * left_at[:, :1].astype(F32)
        scale = sigma_scale if q == 0 else 1.0
        start = jnp.broadcast_to(start * scale, (2 * SUB, LANE))
        step = jnp.broadcast_to(step * (scale * (knots - 1)), (2 * SUB, LANE))
        coef[4 * q] = start[:SUB]
        coef[4 * q + 1] = start[SUB:]
        coef[4 * q + 2] = step[:SUB]
        coef[4 * q + 3] = step[SUB:]


def threshold_of(knots):
    edge = np.float32(SUB / (knots - 1.0))
    scale = np.float32(knots - 1.0)
    while edge * scale >= SUB:
        edge = np.nextafter(edge, np.float32(0.0))
    while edge * scale < SUB:
        edge = np.nextafter(edge, np.float32(1.0))
    return float(edge)


def place_of(cells, knots):
    knot = (cells * (knots - 1.0)).astype(jnp.int32)
    return knot & (SUB - 1), cells >= threshold_of(knots)


def value_at(table, place, cells):
    low, high = place
    start = jnp.where(high, rows_of(table[1], low), rows_of(table[0], low))
    step = jnp.where(high, rows_of(table[3], low), rows_of(table[2], low))
    return start + step * cells


def table_of(coef, q):
    return [coef[4 * q + at] for at in range(4)]


def fetch_tile(density_ref, cells_ref, sems, tile):
    columns = pl.ds(pl.multiple_of(tile * LANE, LANE), LANE)
    return pltpu.make_async_copy(density_ref.at[:, :, columns], cells_ref.at[tile], sems.at[tile])


def sums_kernel(sigma_scale, ratio, bits, split, table_ref, density_ref, *rest):
    if split:
        leaving_ref, cells_ref, sigma_ref, coef, send_ref, keep_ref, clear, sems = rest
    else:
        leaving_ref, cells_ref, sigma_ref, coef, sems = rest
    tiles, layers, slices, _ = cells_ref.shape
    knots = table_ref.shape[1]

    @pl.loop(0, tiles)
    def _(tile):
        fetch_tile(density_ref, cells_ref, sems, tile).start()

    fill_coefficients(table_ref, coef, sigma_scale)
    mine = lax.axis_index("view") & 1 if split else 0
    half = (1 << bits) // 2

    @pl.loop(0, tiles)
    def _(tile):
        fetch_tile(density_ref, cells_ref, sems, tile).wait()
        table = table_of(coef, 0)
        down = [jnp.zeros((SUB, LANE), F32) for _ in range(layers)]
        for block in range(slices // SUB):
            through = jnp.zeros((SUB, LANE), F32)
            for b in range(layers):
                rows = slice(block * SUB, block * SUB + SUB)
                cells = cells_ref[tile, b, rows]
                place = place_of(cells, knots)
                sigma = value_at(table, place, cells)
                sigma_ref[tile, b, rows] = sigma
                through = through + sigma
                down[b] = down[b] + sigma
            if split:
                clear[block] = jnp.exp(through)
        columns = pl.ds(pl.multiple_of(tile * LANE, LANE), LANE)
        for b in range(layers):
            leaving_ref[b : b + 1, columns] = jnp.exp(
                jnp.sum(down[b], axis=0, keepdims=True) * ratio
            )
        if split:
            for q in range(half):
                octet = 2 * bit_reversed(q, bits - 1)
                send_ref[q, tile] = clear[octet + 1 - mine]
                keep_ref[q, tile] = clear[octet + mine]


def fill_lighting(pieces, brick_refs, code_ref, tint_ref, lighting, first, total):
    layers, width = lighting.shape[1:]
    wide = width + 2 * LANE
    place = lax.broadcasted_iota(jnp.int32, (layers, wide), 1) + (first - LANE)
    inside = jnp.logical_and(place >= 0, place < total).astype(F32)
    mine = lax.axis_index("light")
    fronts = [inside] * len(DRIFTS)
    for apart in range(len(brick_refs), 0, -1):
        parts, at = [], first - LANE
        if at < 0:
            parts.append(jnp.zeros((layers, -at), F32))
            at = 0
        for (low, high), ref in zip(pieces, brick_refs[apart - 1]):
            stop = min(high, first + width + LANE)
            if at < stop and at >= low:
                parts.append(ref[:, at - low : stop - low])
                at = stop
        if at < first + width + LANE:
            parts.append(jnp.zeros((layers, first + width + LANE - at), F32))
        leaving = jnp.concatenate(parts, axis=1)
        active = mine >= apart
        result = []
        shared = None
        for drift, front in zip(DRIFTS, fronts):
            if shared is None or apart < len(brick_refs):
                row = front * leaving
                shared = 0.5 * row + 0.25 * (pltpu.roll(row, 1, 1) + pltpu.roll(row, wide - 1, 1))
            moved = shared if drift == 0 else pltpu.roll(shared, drift % wide, 1)
            result.append(jnp.where(active, moved * inside, front))
        fronts = result
    for k in range(lighting.shape[0]):
        shade = jnp.zeros((layers, wide), F32)
        for drift, front in zip(DRIFTS, fronts):
            tint = 0.0
            for light in range(tint_ref.shape[0]):
                tint = tint + jnp.where(code_ref[light] == drift, tint_ref[light, k], 0.0)
            shade = shade + tint * front
        lighting[k] = shade[:, LANE : LANE + width]


def weights_of(cell_refs, tile, b, ahead, ratio, knots):
    steps = len(ahead)
    sublane = lax.broadcasted_iota(jnp.int32, (SUB, LANE), 0)
    cells_ref, sigma_ref = cell_refs
    cells, places, sigma = [], [], []
    before, running = [], None
    for j in range(steps):
        rows = pl.ds(j, SUB, stride=steps)
        cells.append(cells_ref[tile, b, rows, :])
        places.append(place_of(cells[j], knots))
        sigma.append(sigma_ref[tile, b, rows, :])
        before.append(running)
        running = sigma[j] if running is None else running + sigma[j]
    earlier = running
    for hop in (1, 2, 4):
        earlier = earlier + jnp.where(sublane >= hop, pltpu.roll(earlier, hop, 0), 0.0)
    earlier = earlier - running
    weights = []
    for j in range(steps):
        inside = earlier if j == 0 else earlier + before[j]
        shadow = jnp.exp(inside * ratio)
        passed = jnp.exp(sigma[j])
        if ahead[j] is None:
            after = passed
            weights.append((1.0 - passed) * shadow)
        else:
            after = ahead[j] * passed
            weights.append((ahead[j] - after) * shadow)
        ahead[j] = after
    return cells, places, weights


def put_halves(send_ref, keep_ref, sums, tile, bits):
    mine = lax.axis_index("view") & 1
    for q in range(1 << bits - 1):
        octet = 2 * bit_reversed(q, bits - 1)
        for k in range(send_ref.shape[1]):
            send_ref[q, k, tile] = sums[k, pl.ds(octet + 1 - mine, SUB, stride=SUB), :]
            keep_ref[q, k, tile] = sums[k, pl.ds(octet + mine, SUB, stride=SUB), :]


def shade_kernel(
    ratio, knots, first, total, bits, pieces, far, late, whole_out,
    code_ref, tint_ref, coef, *rest,
):
    cell_refs, rest = rest[:2], rest[2:]
    brick_refs = [rest[at * len(pieces) : (at + 1) * len(pieces)] for at in range(far)]
    rest = rest[far * len(pieces) + late :]
    if whole_out:
        out_ref, lighting, sums = rest
    else:
        send_ref, keep_ref, lighting, sums = rest
    layers, slices = cell_refs[0].shape[1:3]
    steps = slices // SUB
    channels = lighting.shape[0]
    fill_lighting(pieces, brick_refs, code_ref, tint_ref, lighting, first, total)

    @pl.loop(0, lighting.shape[2] // LANE)
    def _(tile):
        columns = pl.ds(pl.multiple_of(tile * LANE, LANE), LANE)
        ahead = [None] * steps
        for b in range(layers):
            cells, places, weights = weights_of(
                cell_refs, first // LANE + tile, b, ahead, ratio, knots
            )
            for k in range(channels):
                lit = jnp.broadcast_to(lighting[k, b : b + 1, columns], (SUB, LANE))
                table = [entry * lit for entry in table_of(coef, k + 1)]
                for j in range(steps):
                    rows = pl.ds(j * SUB, SUB)
                    term = value_at(table, places[j], cells[j]) * weights[j]
                    if b == 0:
                        sums[k, rows] = term
                    else:
                        sums[k, rows] = sums[k, rows] + term
        if whole_out:
            for j in range(steps):
                sums[channels, pl.ds(j * SUB, SUB)] = ahead[j]
            for octet in range(SUB):
                for k in range(channels + 1):
                    for part in range(steps // SUB):
                        out_ref[k, tile, pl.ds(octet * steps + part * SUB, SUB)] = sums[
                            k, pl.ds(part * SUB * SUB + octet, SUB, stride=SUB), :
                        ]
        else:
            put_halves(send_ref, keep_ref, sums, tile, bits)


def unlit_kernel(ratio, knots, first, late, coef, *rest):
    cell_refs, out_ref = rest[:2], rest[2 + late]
    tiles, layers, channels, slices, _ = out_ref.shape
    steps = slices // SUB

    @pl.loop(0, tiles)
    def _(tile):
        ahead = [None] * steps
        for b in range(layers):
            cells, places, weights = weights_of(
                cell_refs, first // LANE + tile, b, ahead, ratio, knots
            )
            for k in range(channels):
                table = table_of(coef, k + 1)
                for j in range(steps):
                    term = value_at(table, places[j], cells[j]) * weights[j]
                    out_ref[tile, b, k, j * SUB : j * SUB + SUB] = term


def lit_kernel(first, total, bits, pieces, far, late, code_ref, tint_ref, unlit_ref, *rest):
    brick_refs = [rest[at * len(pieces) : (at + 1) * len(pieces)] for at in range(far)]
    send_ref, keep_ref, lighting, sums = rest[far * len(pieces) + late :]
    tiles, layers, channels, slices, _ = unlit_ref.shape
    fill_lighting(pieces, brick_refs, code_ref, tint_ref, lighting, first, total)

    @pl.loop(0, tiles)
    def _(tile):
        columns = pl.ds(pl.multiple_of(tile * LANE, LANE), LANE)
        for k in range(channels):
            lit = [
                jnp.broadcast_to(lighting[k, b : b + 1, columns], (SUB, LANE))
                for b in range(layers)
            ]
            for j in range(slices // SUB):
                rows = slice(j * SUB, j * SUB + SUB)
                terms = [unlit_ref[tile, b, k, rows] * lit[b] for b in range(layers)]
                sums[k, rows] = functools.reduce(jnp.add, terms)
        put_halves(send_ref, keep_ref, sums, tile, bits)


VMEM = functools.partial(pl.BlockSpec, memory_space=pltpu.VMEM)
SMEM = functools.partial(pl.BlockSpec, memory_space=pltpu.SMEM)
ANY = functools.partial(pl.BlockSpec, memory_space=pl.ANY)
HBM = functools.partial(pl.BlockSpec, memory_space=pltpu.HBM)


def shape(*dims):
    return jax.ShapeDtypeStruct(dims, F32)


def cost(cells, columns, per_cell):
    count = cells.shape[1] * cells.shape[2] * columns
    return pl.CostEstimate(flops=count * per_cell, bytes_accessed=4 * count, transcendentals=0)


MERGE_COST = pl.CostEstimate(flops=2 * 10**10, bytes_accessed=2**20, transcendentals=0)


def sums(density, table, sigma_scale, ratio, bits, split):
    layers, slices, total = density.shape
    tiles = total // LANE
    half = (1 << bits) // 2
    outs = [
        shape(layers, total),
        shape(tiles, layers, slices, LANE),
        shape(tiles, layers, slices, LANE),
        shape(4 * table.shape[0], SUB, LANE),
    ]
    cells_shape = outs[1]
    scratch = []
    if split:
        outs += [shape(half, tiles, SUB, LANE)] * 2
        scratch.append(pltpu.VMEM((slices // SUB, SUB, LANE), F32))
    scratch.append(pltpu.SemaphoreType.DMA((tiles,)))
    return pl.pallas_call(
        functools.partial(sums_kernel, sigma_scale, ratio, bits, split),
        in_specs=[VMEM(), HBM()],
        out_specs=[VMEM()] * len(outs),
        out_shape=outs,
        scratch_shapes=scratch,
        compiler_params=params(STREAM_LIMIT),
        cost_estimate=cost(cells_shape, total, 4000),
        name="sums",
    )(table, density)


def shade(coef, cells, knots, code, tint, bricks, pieces, low, high, ratio, bits, whole_out, after=()):
    tiles, layers, slices, _ = cells[0].shape
    channels = tint.shape[1]
    half = (1 << bits) // 2
    if whole_out:
        outs = [shape(channels + 1, (high - low) // LANE, slices, LANE)]
    else:
        outs = [shape(half, channels, (high - low) // LANE, SUB, LANE)] * 2
    operands = [row for rows in bricks for row in rows]
    return pl.pallas_call(
        functools.partial(
            shade_kernel, ratio, knots, low, tiles * LANE, bits, pieces, len(bricks), len(after),
            whole_out,
        ),
        in_specs=[SMEM()] * 2 + [VMEM()] * (3 + len(operands)) + [ANY()] * len(after),
        out_specs=[VMEM()] * len(outs),
        out_shape=outs,
        scratch_shapes=[
            pltpu.VMEM((channels, layers, high - low), F32),
            pltpu.VMEM((channels + 1, slices, LANE), F32),
        ],
        compiler_params=params(),
        cost_estimate=cost(cells[0], high - low, 10000),
        name="shade",
    )(code, tint, coef, *cells, *operands, *after)


def unlit(coef, cells, knots, channels, low, high, ratio, after=()):
    layers, slices = cells[0].shape[1:3]
    return pl.pallas_call(
        functools.partial(unlit_kernel, ratio, knots, low, len(after)),
        in_specs=[VMEM()] * 3 + [ANY()] * len(after),
        out_specs=VMEM(),
        out_shape=shape((high - low) // LANE, layers, channels, slices, LANE),
        compiler_params=params(),
        cost_estimate=cost(cells[0], high - low, 10000),
        name="unlit",
    )(coef, *cells, *after)


def lit(cells, code, tint, bricks, pieces, low, high, total, bits, after=()):
    tiles, layers, channels, slices, _ = cells.shape
    half = (1 << bits) // 2
    operands = [row for rows in bricks for row in rows]
    return pl.pallas_call(
        functools.partial(
            lit_kernel, low, total, bits, pieces, len(bricks), len(after)
        ),
        in_specs=[SMEM()] * 2 + [VMEM()] * (1 + len(operands)) + [ANY()] * len(after),
        out_specs=[VMEM()] * 2,
        out_shape=[shape(half, channels, tiles, SUB, LANE)] * 2,
        scratch_shapes=[
            pltpu.VMEM((channels, layers, high - low), F32),
            pltpu.VMEM((channels, slices, LANE), F32),
        ],
        compiler_params=params(),
        name="lit",
    )(code, tint, cells, *operands, *after)


def merge_clear_kernel(bit, own_ref, other_ref, *rest):
    send_ref, keep_ref = rest[-2:]
    half = send_ref.shape[0]
    mine = lax.axis_index("view") >> bit + 1 & 1
    for at in range(half):
        there, here = (1 - mine) * half + at, mine * half + at
        send_ref[at] = own_ref[there] * other_ref[there]
        keep_ref[at] = own_ref[here] * other_ref[here]


def merge_clear(own, other, bit, after=()):
    half = shape(own.shape[0] // 2, *own.shape[1:])
    return pl.pallas_call(
        functools.partial(merge_clear_kernel, bit),
        in_specs=[VMEM()] * 2 + [ANY()] * len(after),
        out_specs=[VMEM()] * 2,
        out_shape=[half] * 2,
        compiler_params=params(),
        cost_estimate=MERGE_COST,
        name="merge_clear",
    )(own, other, *after)


def merge_kernel(bit, start, parts, *refs):
    owns, others = refs[:parts], refs[parts : 2 * parts]
    own_clear_ref, other_clear_ref, *rest = refs[2 * parts :]
    send_ref, keep_ref = rest[-2:]
    half, channels = keep_ref.shape[:2]
    me = lax.axis_index("view")
    mine = me >> bit + 1 & 1

    def merged(fronts, backs, clear_ref):
        offset = 0
        for front_ref, back_ref in zip(fronts, backs):
            count = front_ref.shape[2]
            tiles, to = pl.ds(start + offset, count), pl.ds(offset, count)
            for at in range(half):
                for to_ref, side in ((send_ref, 1 - mine), (keep_ref, mine)):
                    source = side * half + at
                    clear = clear_ref[source, tiles]
                    for k in range(channels):
                        value = front_ref[source, k] + clear * back_ref[source, k]
                        to_ref[at, k, to] = value
            offset += count

    upper = me >> bit & 1 == 1

    @pl.when(upper)
    def _():
        merged(others, owns, other_clear_ref)

    @pl.when(jnp.logical_not(upper))
    def _():
        merged(owns, others, own_clear_ref)


def merge(owns, others, own_clear, other_clear, bit, low, after=()):
    count, channels = owns[0].shape[:2]
    tiles = sum(own.shape[2] for own in owns)
    half = shape(count // 2, channels, tiles, SUB, LANE)
    outs = [half] * 2
    return pl.pallas_call(
        functools.partial(merge_kernel, bit, low // LANE, len(owns)),
        in_specs=[VMEM()] * (2 * len(owns) + 2) + [ANY()] * len(after),
        out_specs=[VMEM()] * len(outs),
        out_shape=outs,
        compiler_params=params(),
        cost_estimate=MERGE_COST,
        name="merge",
    )(*owns, *others, own_clear, other_clear, *after)


def last_kernel(bit, firsts, *refs):
    chunks = len(firsts)
    owns, others = refs[:chunks], refs[chunks : 2 * chunks]
    own_clear_ref, other_clear_ref, image_ref = refs[2 * chunks :]
    channels = owns[0].shape[1]
    upper = lax.axis_index("view") >> bit & 1 == 1

    def merged(swapped):
        for at, first in enumerate(firsts):
            for tile in range(owns[at].shape[2]):
                columns = slice(first + tile * LANE, first + tile * LANE + LANE)
                whole = first // LANE + tile
                clear = (other_clear_ref if swapped else own_clear_ref)[0, whole]
                for k in range(channels):
                    own, other = owns[at][0, k, tile], others[at][0, k, tile]
                    front, back = (other, own) if swapped else (own, other)
                    image_ref[k, :, columns] = front + clear * back

    for tile in range(own_clear_ref.shape[1]):
        columns = slice(tile * LANE, tile * LANE + LANE)
        image_ref[channels, :, columns] = own_clear_ref[0, tile] * other_clear_ref[0, tile]

    @pl.when(upper)
    def _():
        merged(True)

    @pl.when(jnp.logical_not(upper))
    def _():
        merged(False)


def last(owns, others, own_clear, other_clear, bit, firsts, total):
    return pl.pallas_call(
        functools.partial(last_kernel, bit, firsts),
        in_specs=[VMEM()] * (2 * len(owns) + 2),
        out_specs=VMEM(),
        out_shape=shape(owns[0].shape[1] + 1, SUB, total),
        compiler_params=params(),
        name="last",
    )(*owns, *others, own_clear, other_clear)


def swap(block, bit):
    count = lax.axis_size("view")
    return lax.ppermute(block, "view", [(at, at ^ 1 << bit) for at in range(count)])


def from_earlier(leaving):
    count = lax.axis_size("light")
    return [
        lax.ppermute(leaving, "light", [(at, at + apart) for at in range(count - apart)])
        for apart in range(1, count)
    ]


def composite_over(front, back):
    clear = front[-1:]
    return jnp.concatenate([front[:-1] + clear * back[:-1], clear * back[-1:]])


def plain(density, table, light_code, light_tint, sigma_scale, ratio, bits):
    slices, total = density.shape[1:]
    leaving, *cells, coef = sums(density, table, sigma_scale, ratio, 0, False)
    bricks = [[row] for row in from_earlier(leaving)]
    parts = shade(
        coef, cells, table.shape[1], light_code, light_tint, bricks, [(0, total)], 0, total, ratio,
        0, True,
    )[0]
    rows = slices >> bits
    depth = parts.shape[0]
    current = parts.transpose(0, 2, 1, 3).reshape((depth,) + (2,) * bits + (rows, total))
    current = current.transpose((0,) + tuple(range(bits, 0, -1)) + (bits + 1, bits + 2))
    for bit in range(bits):
        upper = lax.axis_index("view") >> bit & 1 == 1
        first, second = current[:, 0], current[:, 1]
        kept = jnp.where(upper, second, first)
        arrived = swap(jnp.where(upper, first, second), bit)
        current = composite_over(jnp.where(upper, arrived, kept), jnp.where(upper, kept, arrived))
    return current.reshape(depth, rows, total)


PARTS = ((11,), (12,), (9,))


def ranges(total):
    whole = sum(sum(parts) for parts in PARTS)
    result, done = [], 0
    for parts in PARTS:
        result.append([])
        for part in parts:
            low = total * done // (whole * LANE) * LANE
            done += part
            result[-1].append((low, total * done // (whole * LANE) * LANE))
    return result


def local(density, tables, table_index, light_code, light_tint):
    layers, slices, total = density.shape
    views = lax.axis_size("view")
    bits = views.bit_length() - 1
    sigma_scale = -1.0 / (layers * views)
    ratio = layers * views / (slices * lax.axis_size("light"))
    chosen = lax.broadcasted_iota(jnp.int32, (tables.shape[0], 1), 0) == table_index
    table = jnp.sum(jnp.where(chosen[:, :, None], tables, 0.0), axis=0)
    if views * SUB != slices or bits != 3:
        return plain(density, table, light_code, light_tint, sigma_scale, ratio, bits)
    pieces = [(0, total)]
    chunks = ranges(total)
    knots = table.shape[1]
    leaving, *cells, coef, send, keep = sums(
        density, table, sigma_scale, ratio, bits, True
    )
    bricks = [[row] for row in from_earlier(leaving)]
    clear = [(keep, swap(send, 0))]
    send, keep = merge_clear(*clear[0], 0)
    clear.append((keep, swap(send, 1)))
    first = unlit(coef, cells, knots, light_tint.shape[1], *chunks[0][0], ratio, after=(send,))
    done = lit(first, light_code, light_tint, bricks, pieces, *chunks[0][0], total, bits)
    halves = [(done[1], swap(done[0], 0))]
    clear_send, own_clear = merge_clear(*clear[1], 1, after=(done[0],))
    clear.append((own_clear, swap(clear_send, 2)))
    done = clear_send
    state = []

    def forward(after):
        at = len(state) - 1
        settled = state[at - 1][1] if at else clear[2][1]
        send, keep = merge(
            [state[at][0]], [state[at][1]], *clear[1], 1, chunks[at][0][0], after=(after, settled)
        )
        state[at] = (keep, swap(send, 2))
        return send

    for at, parts in enumerate(chunks):
        for number, (low, high) in enumerate(parts):
            if at:
                send, keep = shade(
                    coef, cells, knots, light_code, light_tint, bricks, pieces, low, high, ratio,
                    bits, False, after=(done,),
                )
                halves.append((keep, swap(send, 0)))
                done = send
                if number == 0:
                    done = forward(done)
        send, keep = merge(*zip(*halves), *clear[0], 0, parts[0][0], after=(done,))
        halves = []
        done = send
        state.append((keep, swap(send, 1)))
    forward(done)
    owns, others = zip(*state)
    return last(owns, others, *clear[2], 2, [parts[0][0] for parts in chunks], total)


def solution(mesh):
    return jax.shard_map(
        local,
        mesh=mesh,
        in_specs=(P("view", "light", None), P(), P("light", "view"), P(), P()),
        out_specs=P(None, ("light", "view"), None),
        check_vma=False,
    )
```

```python
import functools

import jax
import jax.numpy as jnp
import numpy as np
from jax import lax
from jax.experimental import pallas as pl
from jax.experimental.pallas import tpu as pltpu
from jax.sharding import PartitionSpec as P

LANE = 128
SUB = 8
DRIFTS = (-1, 0, 1)
VMEM_LIMIT = 16 * 2**20
STREAM_LIMIT = 36 * 2**20
F32 = jnp.float32


def params(limit=VMEM_LIMIT):
    return pltpu.CompilerParams(vmem_limit_bytes=limit)


def bit_reversed(value, bits):
    return sum((value >> at & 1) << bits - 1 - at for at in range(bits))


def rows_of(table, index):
    return jnp.take_along_axis(table, index, axis=0, mode="promise_in_bounds")


def fill_coefficients(index_ref, tables_ref, coef, sigma_scale):
    rows = jnp.zeros(tables_ref.shape[1:], F32)
    for at in range(tables_ref.shape[0]):
        chosen = jnp.broadcast_to(index_ref[...], rows.shape) == at
        rows = jnp.where(chosen, tables_ref[at], rows)
    knots = rows.shape[1]
    at_row = lax.broadcasted_iota(jnp.int32, (2 * SUB, knots), 0)
    at_col = lax.broadcasted_iota(jnp.int32, (2 * SUB, knots), 1)
    left_at = jnp.minimum(at_row, knots - 2)
    for q in range(rows.shape[0]):
        row = jnp.broadcast_to(rows[q : q + 1], (2 * SUB, knots))
        left = jnp.sum(jnp.where(at_col == left_at, row, 0.0), axis=1, keepdims=True)
        right = jnp.sum(jnp.where(at_col == left_at + 1, row, 0.0), axis=1, keepdims=True)
        step = right - left
        start = left - step * left_at[:, :1].astype(F32)
        scale = sigma_scale if q == 0 else 1.0
        start = jnp.broadcast_to(start * scale, (2 * SUB, LANE))
        step = jnp.broadcast_to(step * (scale * (knots - 1)), (2 * SUB, LANE))
        coef[4 * q] = start[:SUB]
        coef[4 * q + 1] = start[SUB:]
        coef[4 * q + 2] = step[:SUB]
        coef[4 * q + 3] = step[SUB:]


def threshold_of(knots):
    edge = np.float32(SUB / (knots - 1.0))
    scale = np.float32(knots - 1.0)
    while edge * scale >= SUB:
        edge = np.nextafter(edge, np.float32(0.0))
    while edge * scale < SUB:
        edge = np.nextafter(edge, np.float32(1.0))
    return float(edge)


def place_of(cells, knots):
    knot = (cells * (knots - 1.0)).astype(jnp.int32)
    return knot & (SUB - 1), cells >= threshold_of(knots)


def value_at(table, place, cells):
    low, high = place
    start = jnp.where(high, rows_of(table[1], low), rows_of(table[0], low))
    step = jnp.where(high, rows_of(table[3], low), rows_of(table[2], low))
    return start + step * cells


def table_of(coef, q):
    return [coef[4 * q + at] for at in range(4)]


def fetch_tile(density_ref, cells_ref, sems, tile):
    columns = pl.ds(pl.multiple_of(tile * LANE, LANE), LANE)
    return pltpu.make_async_copy(density_ref.at[:, :, columns], cells_ref.at[tile], sems.at[tile])


def sums_kernel(sigma_scale, ratio, bits, split, index_ref, tables_ref, density_ref, *rest):
    if split:
        leaving_ref, cells_ref, sigma_ref, coef, send_ref, keep_ref, clear, sems = rest
    else:
        leaving_ref, cells_ref, sigma_ref, coef, sems = rest
    tiles, layers, slices, _ = cells_ref.shape
    knots = tables_ref.shape[2]

    @pl.loop(0, tiles)
    def _(tile):
        fetch_tile(density_ref, cells_ref, sems, tile).start()

    fill_coefficients(index_ref, tables_ref, coef, sigma_scale)
    mine = lax.axis_index("view") & 1 if split else 0
    half = (1 << bits) // 2

    @pl.loop(0, tiles)
    def _(tile):
        fetch_tile(density_ref, cells_ref, sems, tile).wait()
        table = table_of(coef, 0)
        down = [jnp.zeros((SUB, LANE), F32) for _ in range(layers)]
        for block in range(slices // SUB):
            through = jnp.zeros((SUB, LANE), F32)
            for b in range(layers):
                rows = slice(block * SUB, block * SUB + SUB)
                cells = cells_ref[tile, b, rows]
                place = place_of(cells, knots)
                sigma = value_at(table, place, cells)
                sigma_ref[tile, b, rows] = sigma
                through = through + sigma
                down[b] = down[b] + sigma
            if split:
                clear[block] = jnp.exp(through)
        columns = pl.ds(pl.multiple_of(tile * LANE, LANE), LANE)
        for b in range(layers):
            leaving_ref[b : b + 1, columns] = jnp.exp(
                jnp.sum(down[b], axis=0, keepdims=True) * ratio
            )
        if split:
            for q in range(half):
                octet = 2 * bit_reversed(q, bits - 1)
                send_ref[q, tile] = clear[octet + 1 - mine]
                keep_ref[q, tile] = clear[octet + mine]


def fill_lighting(pieces, brick_refs, code_ref, tint_ref, lighting, first, total):
    layers, width = lighting.shape[1:]
    wide = width + 2 * LANE
    place = lax.broadcasted_iota(jnp.int32, (layers, wide), 1) + (first - LANE)
    inside = jnp.logical_and(place >= 0, place < total).astype(F32)
    mine = lax.axis_index("light")
    fronts = [inside] * len(DRIFTS)
    for apart in range(len(brick_refs), 0, -1):
        parts, at = [], first - LANE
        if at < 0:
            parts.append(jnp.zeros((layers, -at), F32))
            at = 0
        for (low, high), ref in zip(pieces, brick_refs[apart - 1]):
            stop = min(high, first + width + LANE)
            if at < stop and at >= low:
                parts.append(ref[:, at - low : stop - low])
                at = stop
        if at < first + width + LANE:
            parts.append(jnp.zeros((layers, first + width + LANE - at), F32))
        leaving = jnp.concatenate(parts, axis=1)
        active = mine >= apart
        result = []
        for drift, front in zip(DRIFTS, fronts):
            row = front * leaving
            taps = [
                row if hop % wide == 0 else pltpu.roll(row, hop % wide, 1)
                for hop in (drift - 1, drift, drift + 1)
            ]
            moved = 0.5 * taps[1] + 0.25 * (taps[0] + taps[2])
            result.append(jnp.where(active, moved * inside, front))
        fronts = result
    for k in range(lighting.shape[0]):
        shade = jnp.zeros((layers, wide), F32)
        for drift, front in zip(DRIFTS, fronts):
            tint = 0.0
            for light in range(tint_ref.shape[0]):
                tint = tint + jnp.where(code_ref[light] == drift, tint_ref[light, k], 0.0)
            shade = shade + tint * front
        lighting[k] = shade[:, LANE : LANE + width]


def weights_of(cell_refs, tile, b, ahead, ratio, knots):
    steps = len(ahead)
    sublane = lax.broadcasted_iota(jnp.int32, (SUB, LANE), 0)
    cells_ref, sigma_ref = cell_refs
    cells, places, sigma = [], [], []
    before, running = [], None
    for j in range(steps):
        rows = pl.ds(j, SUB, stride=steps)
        cells.append(cells_ref[tile, b, rows, :])
        places.append(place_of(cells[j], knots))
        sigma.append(sigma_ref[tile, b, rows, :])
        before.append(running)
        running = sigma[j] if running is None else running + sigma[j]
    earlier = running
    for hop in (1, 2, 4):
        earlier = earlier + jnp.where(sublane >= hop, pltpu.roll(earlier, hop, 0), 0.0)
    earlier = earlier - running
    weights = []
    for j in range(steps):
        inside = earlier if j == 0 else earlier + before[j]
        shadow = jnp.exp(inside * ratio)
        passed = jnp.exp(sigma[j])
        if ahead[j] is None:
            after = passed
            weights.append((1.0 - passed) * shadow)
        else:
            after = ahead[j] * passed
            weights.append((ahead[j] - after) * shadow)
        ahead[j] = after
    return cells, places, weights


def put_halves(send_ref, keep_ref, sums, tile, bits):
    mine = lax.axis_index("view") & 1
    for q in range(1 << bits - 1):
        octet = 2 * bit_reversed(q, bits - 1)
        for k in range(send_ref.shape[1]):
            send_ref[q, k, tile] = sums[k, pl.ds(octet + 1 - mine, SUB, stride=SUB), :]
            keep_ref[q, k, tile] = sums[k, pl.ds(octet + mine, SUB, stride=SUB), :]


def shade_kernel(
    ratio, knots, first, total, bits, pieces, far, late, whole_out,
    code_ref, tint_ref, coef, *rest,
):
    cell_refs, rest = rest[:2], rest[2:]
    brick_refs = [rest[at * len(pieces) : (at + 1) * len(pieces)] for at in range(far)]
    rest = rest[far * len(pieces) + late :]
    if whole_out:
        out_ref, lighting, sums = rest
    else:
        send_ref, keep_ref, lighting, sums = rest
    layers, slices = cell_refs[0].shape[1:3]
    steps = slices // SUB
    channels = lighting.shape[0]
    fill_lighting(pieces, brick_refs, code_ref, tint_ref, lighting, first, total)

    @pl.loop(0, lighting.shape[2] // LANE)
    def _(tile):
        columns = pl.ds(pl.multiple_of(tile * LANE, LANE), LANE)
        ahead = [None] * steps
        for b in range(layers):
            cells, places, weights = weights_of(
                cell_refs, first // LANE + tile, b, ahead, ratio, knots
            )
            for k in range(channels):
                lit = jnp.broadcast_to(lighting[k, b : b + 1, columns], (SUB, LANE))
                table = [entry * lit for entry in table_of(coef, k + 1)]
                for j in range(steps):
                    rows = pl.ds(j * SUB, SUB)
                    term = value_at(table, places[j], cells[j]) * weights[j]
                    if b == 0:
                        sums[k, rows] = term
                    else:
                        sums[k, rows] = sums[k, rows] + term
        if whole_out:
            for j in range(steps):
                sums[channels, pl.ds(j * SUB, SUB)] = ahead[j]
            for octet in range(SUB):
                for k in range(channels + 1):
                    for part in range(steps // SUB):
                        out_ref[k, tile, pl.ds(octet * steps + part * SUB, SUB)] = sums[
                            k, pl.ds(part * SUB * SUB + octet, SUB, stride=SUB), :
                        ]
        else:
            put_halves(send_ref, keep_ref, sums, tile, bits)


def unlit_kernel(ratio, knots, first, late, coef, *rest):
    cell_refs, out_ref = rest[:2], rest[2 + late]
    tiles, layers, channels, slices, _ = out_ref.shape
    steps = slices // SUB

    @pl.loop(0, tiles)
    def _(tile):
        ahead = [None] * steps
        for b in range(layers):
            cells, places, weights = weights_of(
                cell_refs, first // LANE + tile, b, ahead, ratio, knots
            )
            for k in range(channels):
                table = table_of(coef, k + 1)
                for j in range(steps):
                    term = value_at(table, places[j], cells[j]) * weights[j]
                    out_ref[tile, b, k, j * SUB : j * SUB + SUB] = term


def lit_kernel(first, total, bits, pieces, far, late, code_ref, tint_ref, unlit_ref, *rest):
    brick_refs = [rest[at * len(pieces) : (at + 1) * len(pieces)] for at in range(far)]
    send_ref, keep_ref, lighting, sums = rest[far * len(pieces) + late :]
    tiles, layers, channels, slices, _ = unlit_ref.shape
    fill_lighting(pieces, brick_refs, code_ref, tint_ref, lighting, first, total)

    @pl.loop(0, tiles)
    def _(tile):
        columns = pl.ds(pl.multiple_of(tile * LANE, LANE), LANE)
        for k in range(channels):
            lit = [
                jnp.broadcast_to(lighting[k, b : b + 1, columns], (SUB, LANE))
                for b in range(layers)
            ]
            for j in range(slices // SUB):
                rows = slice(j * SUB, j * SUB + SUB)
                terms = [unlit_ref[tile, b, k, rows] * lit[b] for b in range(layers)]
                sums[k, rows] = functools.reduce(jnp.add, terms)
        put_halves(send_ref, keep_ref, sums, tile, bits)


VMEM = functools.partial(pl.BlockSpec, memory_space=pltpu.VMEM)
SMEM = functools.partial(pl.BlockSpec, memory_space=pltpu.SMEM)
ANY = functools.partial(pl.BlockSpec, memory_space=pl.ANY)
HBM = functools.partial(pl.BlockSpec, memory_space=pltpu.HBM)


def shape(*dims):
    return jax.ShapeDtypeStruct(dims, F32)


def cost(cells, columns, per_cell):
    count = cells.shape[1] * cells.shape[2] * columns
    return pl.CostEstimate(flops=count * per_cell, bytes_accessed=4 * count, transcendentals=0)


MERGE_COST = pl.CostEstimate(flops=2 * 10**10, bytes_accessed=2**20, transcendentals=0)


def sums(density, tables, index, sigma_scale, ratio, bits, split):
    layers, slices, total = density.shape
    tiles = total // LANE
    half = (1 << bits) // 2
    outs = [
        shape(layers, total),
        shape(tiles, layers, slices, LANE),
        shape(tiles, layers, slices, LANE),
        shape(4 * tables.shape[1], SUB, LANE),
    ]
    cells_shape = outs[1]
    scratch = []
    if split:
        outs += [shape(half, tiles, SUB, LANE)] * 2
        scratch.append(pltpu.VMEM((slices // SUB, SUB, LANE), F32))
    scratch.append(pltpu.SemaphoreType.DMA((tiles,)))
    return pl.pallas_call(
        functools.partial(sums_kernel, sigma_scale, ratio, bits, split),
        in_specs=[VMEM(), VMEM(), HBM()],
        out_specs=[VMEM()] * len(outs),
        out_shape=outs,
        scratch_shapes=scratch,
        compiler_params=params(STREAM_LIMIT),
        cost_estimate=cost(cells_shape, total, 4000),
        name="sums",
    )(index, tables, density)


def shade(coef, cells, knots, code, tint, bricks, pieces, low, high, ratio, bits, whole_out, after=()):
    tiles, layers, slices, _ = cells[0].shape
    channels = tint.shape[1]
    half = (1 << bits) // 2
    if whole_out:
        outs = [shape(channels + 1, (high - low) // LANE, slices, LANE)]
    else:
        outs = [shape(half, channels, (high - low) // LANE, SUB, LANE)] * 2
    operands = [row for rows in bricks for row in rows]
    return pl.pallas_call(
        functools.partial(
            shade_kernel, ratio, knots, low, tiles * LANE, bits, pieces, len(bricks), len(after),
            whole_out,
        ),
        in_specs=[SMEM()] * 2 + [VMEM()] * (3 + len(operands)) + [ANY()] * len(after),
        out_specs=[VMEM()] * len(outs),
        out_shape=outs,
        scratch_shapes=[
            pltpu.VMEM((channels, layers, high - low), F32),
            pltpu.VMEM((channels + 1, slices, LANE), F32),
        ],
        compiler_params=params(),
        cost_estimate=cost(cells[0], high - low, 10000),
        name="shade",
    )(code, tint, coef, *cells, *operands, *after)


def unlit(coef, cells, knots, channels, low, high, ratio, after=()):
    layers, slices = cells[0].shape[1:3]
    return pl.pallas_call(
        functools.partial(unlit_kernel, ratio, knots, low, len(after)),
        in_specs=[VMEM()] * 3 + [ANY()] * len(after),
        out_specs=VMEM(),
        out_shape=shape((high - low) // LANE, layers, channels, slices, LANE),
        compiler_params=params(),
        cost_estimate=cost(cells[0], high - low, 10000),
        name="unlit",
    )(coef, *cells, *after)


def lit(cells, code, tint, bricks, pieces, low, high, total, bits, after=()):
    tiles, layers, channels, slices, _ = cells.shape
    half = (1 << bits) // 2
    operands = [row for rows in bricks for row in rows]
    return pl.pallas_call(
        functools.partial(
            lit_kernel, low, total, bits, pieces, len(bricks), len(after)
        ),
        in_specs=[SMEM()] * 2 + [VMEM()] * (1 + len(operands)) + [ANY()] * len(after),
        out_specs=[VMEM()] * 2,
        out_shape=[shape(half, channels, tiles, SUB, LANE)] * 2,
        scratch_shapes=[
            pltpu.VMEM((channels, layers, high - low), F32),
            pltpu.VMEM((channels, slices, LANE), F32),
        ],
        compiler_params=params(),
        name="lit",
    )(code, tint, cells, *operands, *after)


def merge_clear_kernel(bit, own_ref, other_ref, *rest):
    send_ref, keep_ref = rest[-2:]
    half = send_ref.shape[0]
    mine = lax.axis_index("view") >> bit + 1 & 1
    for at in range(half):
        there, here = (1 - mine) * half + at, mine * half + at
        send_ref[at] = own_ref[there] * other_ref[there]
        keep_ref[at] = own_ref[here] * other_ref[here]


def merge_clear(own, other, bit, after=()):
    half = shape(own.shape[0] // 2, *own.shape[1:])
    return pl.pallas_call(
        functools.partial(merge_clear_kernel, bit),
        in_specs=[VMEM()] * 2 + [ANY()] * len(after),
        out_specs=[VMEM()] * 2,
        out_shape=[half] * 2,
        compiler_params=params(),
        cost_estimate=MERGE_COST,
        name="merge_clear",
    )(own, other, *after)


def merge_kernel(bit, start, parts, *refs):
    owns, others = refs[:parts], refs[parts : 2 * parts]
    own_clear_ref, other_clear_ref, *rest = refs[2 * parts :]
    send_ref, keep_ref = rest[-2:]
    half, channels = keep_ref.shape[:2]
    me = lax.axis_index("view")
    mine = me >> bit + 1 & 1

    def merged(fronts, backs, clear_ref):
        offset = 0
        for front_ref, back_ref in zip(fronts, backs):
            count = front_ref.shape[2]
            tiles, to = pl.ds(start + offset, count), pl.ds(offset, count)
            for at in range(half):
                for to_ref, side in ((send_ref, 1 - mine), (keep_ref, mine)):
                    source = side * half + at
                    clear = clear_ref[source, tiles]
                    for k in range(channels):
                        value = front_ref[source, k] + clear * back_ref[source, k]
                        to_ref[at, k, to] = value
            offset += count

    upper = me >> bit & 1 == 1

    @pl.when(upper)
    def _():
        merged(others, owns, other_clear_ref)

    @pl.when(jnp.logical_not(upper))
    def _():
        merged(owns, others, own_clear_ref)


def merge(owns, others, own_clear, other_clear, bit, low, after=()):
    count, channels = owns[0].shape[:2]
    tiles = sum(own.shape[2] for own in owns)
    half = shape(count // 2, channels, tiles, SUB, LANE)
    outs = [half] * 2
    return pl.pallas_call(
        functools.partial(merge_kernel, bit, low // LANE, len(owns)),
        in_specs=[VMEM()] * (2 * len(owns) + 2) + [ANY()] * len(after),
        out_specs=[VMEM()] * len(outs),
        out_shape=outs,
        compiler_params=params(),
        cost_estimate=MERGE_COST,
        name="merge",
    )(*owns, *others, own_clear, other_clear, *after)


def last_kernel(bit, firsts, *refs):
    chunks = len(firsts)
    owns, others = refs[:chunks], refs[chunks : 2 * chunks]
    own_clear_ref, other_clear_ref, image_ref = refs[2 * chunks :]
    channels = owns[0].shape[1]
    upper = lax.axis_index("view") >> bit & 1 == 1

    def merged(swapped):
        for at, first in enumerate(firsts):
            for tile in range(owns[at].shape[2]):
                columns = slice(first + tile * LANE, first + tile * LANE + LANE)
                whole = first // LANE + tile
                clear = (other_clear_ref if swapped else own_clear_ref)[0, whole]
                for k in range(channels):
                    own, other = owns[at][0, k, tile], others[at][0, k, tile]
                    front, back = (other, own) if swapped else (own, other)
                    image_ref[k, :, columns] = front + clear * back

    for tile in range(own_clear_ref.shape[1]):
        columns = slice(tile * LANE, tile * LANE + LANE)
        image_ref[channels, :, columns] = own_clear_ref[0, tile] * other_clear_ref[0, tile]

    @pl.when(upper)
    def _():
        merged(True)

    @pl.when(jnp.logical_not(upper))
    def _():
        merged(False)


def last(owns, others, own_clear, other_clear, bit, firsts, total):
    return pl.pallas_call(
        functools.partial(last_kernel, bit, firsts),
        in_specs=[VMEM()] * (2 * len(owns) + 2),
        out_specs=VMEM(),
        out_shape=shape(owns[0].shape[1] + 1, SUB, total),
        compiler_params=params(),
        name="last",
    )(*owns, *others, own_clear, other_clear)


def swap(block, bit):
    count = lax.axis_size("view")
    return lax.ppermute(block, "view", [(at, at ^ 1 << bit) for at in range(count)])


def from_earlier(leaving):
    count = lax.axis_size("light")
    return [
        lax.ppermute(leaving, "light", [(at, at + apart) for at in range(count - apart)])
        for apart in range(1, count)
    ]


def composite_over(front, back):
    clear = front[-1:]
    return jnp.concatenate([front[:-1] + clear * back[:-1], clear * back[-1:]])


def plain(density, tables, index, light_code, light_tint, sigma_scale, ratio, bits):
    slices, total = density.shape[1:]
    leaving, *cells, coef = sums(density, tables, index, sigma_scale, ratio, 0, False)
    bricks = [[row] for row in from_earlier(leaving)]
    parts = shade(
        coef, cells, tables.shape[2], light_code, light_tint, bricks, [(0, total)], 0, total, ratio,
        0, True,
    )[0]
    rows = slices >> bits
    depth = parts.shape[0]
    current = parts.transpose(0, 2, 1, 3).reshape((depth,) + (2,) * bits + (rows, total))
    current = current.transpose((0,) + tuple(range(bits, 0, -1)) + (bits + 1, bits + 2))
    for bit in range(bits):
        upper = lax.axis_index("view") >> bit & 1 == 1
        first, second = current[:, 0], current[:, 1]
        kept = jnp.where(upper, second, first)
        arrived = swap(jnp.where(upper, first, second), bit)
        current = composite_over(jnp.where(upper, arrived, kept), jnp.where(upper, kept, arrived))
    return current.reshape(depth, rows, total)


PARTS = ((11,), (12,), (9,))


def ranges(total):
    whole = sum(sum(parts) for parts in PARTS)
    result, done = [], 0
    for parts in PARTS:
        result.append([])
        for part in parts:
            low = total * done // (whole * LANE) * LANE
            done += part
            result[-1].append((low, total * done // (whole * LANE) * LANE))
    return result


def local(density, tables, table_index, light_code, light_tint):
    layers, slices, total = density.shape
    views = lax.axis_size("view")
    bits = views.bit_length() - 1
    sigma_scale = -1.0 / (layers * views)
    ratio = layers * views / (slices * lax.axis_size("light"))
    if views * SUB != slices or bits != 3:
        return plain(
            density, tables, table_index, light_code, light_tint, sigma_scale, ratio, bits
        )
    pieces = [(0, total)]
    chunks = ranges(total)
    knots = tables.shape[2]
    leaving, *cells, coef, send, keep = sums(
        density, tables, table_index, sigma_scale, ratio, bits, True
    )
    bricks = [[row] for row in from_earlier(leaving)]
    clear = [(keep, swap(send, 0))]
    send, keep = merge_clear(*clear[0], 0)
    clear.append((keep, swap(send, 1)))
    first = unlit(coef, cells, knots, light_tint.shape[1], *chunks[0][0], ratio, after=(send,))
    done = lit(first, light_code, light_tint, bricks, pieces, *chunks[0][0], total, bits)
    halves = [(done[1], swap(done[0], 0))]
    clear_send, own_clear = merge_clear(*clear[1], 1, after=(done[0],))
    clear.append((own_clear, swap(clear_send, 2)))
    done = clear_send
    state = []

    def forward(after):
        at = len(state) - 1
        settled = state[at - 1][1] if at else clear[2][1]
        send, keep = merge(
            [state[at][0]], [state[at][1]], *clear[1], 1, chunks[at][0][0], after=(after, settled)
        )
        state[at] = (keep, swap(send, 2))
        return send

    for at, parts in enumerate(chunks):
        for number, (low, high) in enumerate(parts):
            if at:
                send, keep = shade(
                    coef, cells, knots, light_code, light_tint, bricks, pieces, low, high, ratio,
                    bits, False, after=(done,),
                )
                halves.append((keep, swap(send, 0)))
                done = send
                if number == 0:
                    done = forward(done)
        send, keep = merge(*zip(*halves), *clear[0], 0, parts[0][0], after=(done,))
        halves = []
        done = send
        state.append((keep, swap(send, 1)))
    forward(done)
    owns, others = zip(*state)
    return last(owns, others, *clear[2], 2, [parts[0][0] for parts in chunks], total)


def solution(mesh):
    return jax.shard_map(
        local,
        mesh=mesh,
        in_specs=(P("view", "light", None), P(), P("light", "view"), P(), P()),
        out_specs=P(None, ("light", "view"), None),
        check_vma=False,
    )
```

```python
import functools

import jax
import jax.numpy as jnp
import numpy as np
from jax import lax
from jax.experimental import pallas as pl
from jax.experimental.pallas import tpu as pltpu
from jax.sharding import PartitionSpec as P

LANE = 128
SUB = 8
DRIFTS = (-1, 0, 1)
VMEM_LIMIT = 16 * 2**20
STREAM_LIMIT = 36 * 2**20
F32 = jnp.float32


def params(limit=VMEM_LIMIT):
    return pltpu.CompilerParams(vmem_limit_bytes=limit)


def bit_reversed(value, bits):
    return sum((value >> at & 1) << bits - 1 - at for at in range(bits))


def rows_of(table, index):
    return jnp.take_along_axis(table, index, axis=0, mode="promise_in_bounds")


def fill_coefficients(index_ref, tables_ref, coef, sigma_scale):
    rows = jnp.zeros(tables_ref.shape[1:], F32)
    for at in range(tables_ref.shape[0]):
        chosen = jnp.broadcast_to(index_ref[...], rows.shape) == at
        rows = jnp.where(chosen, tables_ref[at], rows)
    knots = rows.shape[1]
    at_row = lax.broadcasted_iota(jnp.int32, (2 * SUB, knots), 0)
    at_col = lax.broadcasted_iota(jnp.int32, (2 * SUB, knots), 1)
    left_at = jnp.minimum(at_row, knots - 2)
    for q in range(rows.shape[0]):
        row = jnp.broadcast_to(rows[q : q + 1], (2 * SUB, knots))
        left = jnp.sum(jnp.where(at_col == left_at, row, 0.0), axis=1, keepdims=True)
        right = jnp.sum(jnp.where(at_col == left_at + 1, row, 0.0), axis=1, keepdims=True)
        step = right - left
        start = left - step * left_at[:, :1].astype(F32)
        scale = sigma_scale if q == 0 else 1.0
        start = jnp.broadcast_to(start * scale, (2 * SUB, LANE))
        step = jnp.broadcast_to(step * (scale * (knots - 1)), (2 * SUB, LANE))
        coef[4 * q] = start[:SUB]
        coef[4 * q + 1] = start[SUB:]
        coef[4 * q + 2] = step[:SUB]
        coef[4 * q + 3] = step[SUB:]


def threshold_of(knots):
    edge = np.float32(SUB / (knots - 1.0))
    scale = np.float32(knots - 1.0)
    while edge * scale >= SUB:
        edge = np.nextafter(edge, np.float32(0.0))
    while edge * scale < SUB:
        edge = np.nextafter(edge, np.float32(1.0))
    return float(edge)


def place_of(cells, knots):
    knot = (cells * (knots - 1.0)).astype(jnp.int32)
    return knot & (SUB - 1), cells >= threshold_of(knots)


def value_at(table, place, cells):
    low, high = place
    start = jnp.where(high, rows_of(table[1], low), rows_of(table[0], low))
    step = jnp.where(high, rows_of(table[3], low), rows_of(table[2], low))
    return start + step * cells


def table_of(coef, q):
    return [coef[4 * q + at] for at in range(4)]


def fetch_tile(density_ref, cells_ref, sems, tile):
    columns = pl.ds(pl.multiple_of(tile * LANE, LANE), LANE)
    return pltpu.make_async_copy(density_ref.at[:, :, columns], cells_ref.at[tile], sems.at[tile])


def sums_kernel(sigma_scale, ratio, bits, split, index_ref, tables_ref, density_ref, *rest):
    if split:
        leaving_ref, cells_ref, sigma_ref, coef, send_ref, keep_ref, clear, sems = rest
    else:
        leaving_ref, cells_ref, sigma_ref, coef, sems = rest
    tiles, layers, slices, _ = cells_ref.shape
    knots = tables_ref.shape[2]

    @pl.loop(0, tiles)
    def _(tile):
        fetch_tile(density_ref, cells_ref, sems, tile).start()

    fill_coefficients(index_ref, tables_ref, coef, sigma_scale)
    mine = lax.axis_index("view") & 1 if split else 0
    half = (1 << bits) // 2

    @pl.loop(0, tiles)
    def _(tile):
        fetch_tile(density_ref, cells_ref, sems, tile).wait()
        table = table_of(coef, 0)
        down = [jnp.zeros((SUB, LANE), F32) for _ in range(layers)]
        for block in range(slices // SUB):
            through = jnp.zeros((SUB, LANE), F32)
            for b in range(layers):
                rows = slice(block * SUB, block * SUB + SUB)
                cells = cells_ref[tile, b, rows]
                place = place_of(cells, knots)
                sigma = value_at(table, place, cells)
                sigma_ref[tile, b, rows] = sigma
                through = through + sigma
                down[b] = down[b] + sigma
            if split:
                clear[block] = jnp.exp(through)
        columns = pl.ds(pl.multiple_of(tile * LANE, LANE), LANE)
        for b in range(layers):
            leaving_ref[b : b + 1, columns] = jnp.exp(
                jnp.sum(down[b], axis=0, keepdims=True) * ratio
            )
        if split:
            for q in range(half):
                octet = 2 * bit_reversed(q, bits - 1)
                send_ref[q, tile] = clear[octet + 1 - mine]
                keep_ref[q, tile] = clear[octet + mine]


def fill_lighting(pieces, brick_refs, code_ref, tint_ref, lighting, first, total):
    layers, width = lighting.shape[1:]
    wide = width + 2 * LANE
    place = lax.broadcasted_iota(jnp.int32, (layers, wide), 1) + (first - LANE)
    inside = jnp.logical_and(place >= 0, place < total).astype(F32)
    within = first >= LANE and first + width + LANE <= total
    mine = lax.axis_index("light")
    fronts = [inside] * len(DRIFTS)
    for apart in range(len(brick_refs), 0, -1):
        parts, at = [], first - LANE
        if at < 0:
            parts.append(jnp.zeros((layers, -at), F32))
            at = 0
        for (low, high), ref in zip(pieces, brick_refs[apart - 1]):
            stop = min(high, first + width + LANE)
            if at < stop and at >= low:
                parts.append(ref[:, at - low : stop - low])
                at = stop
        if at < first + width + LANE:
            parts.append(jnp.zeros((layers, first + width + LANE - at), F32))
        leaving = jnp.concatenate(parts, axis=1)
        active = mine >= apart
        result = []
        for drift, front in zip(DRIFTS, fronts):
            row = front * leaving
            taps = [
                row if hop % wide == 0 else pltpu.roll(row, hop % wide, 1)
                for hop in (drift - 1, drift, drift + 1)
            ]
            moved = 0.5 * taps[1] + 0.25 * (taps[0] + taps[2])
            result.append(jnp.where(active, moved if within else moved * inside, front))
        fronts = result
    for k in range(lighting.shape[0]):
        shade = jnp.zeros((layers, wide), F32)
        for drift, front in zip(DRIFTS, fronts):
            tint = 0.0
            for light in range(tint_ref.shape[0]):
                tint = tint + jnp.where(code_ref[light] == drift, tint_ref[light, k], 0.0)
            shade = shade + tint * front
        lighting[k] = shade[:, LANE : LANE + width]


def weights_of(cell_refs, tile, b, ahead, ratio, knots):
    steps = len(ahead)
    sublane = lax.broadcasted_iota(jnp.int32, (SUB, LANE), 0)
    cells_ref, sigma_ref = cell_refs
    cells, places, sigma = [], [], []
    before, running = [], None
    for j in range(steps):
        rows = pl.ds(j, SUB, stride=steps)
        cells.append(cells_ref[tile, b, rows, :])
        places.append(place_of(cells[j], knots))
        sigma.append(sigma_ref[tile, b, rows, :])
        before.append(running)
        running = sigma[j] if running is None else running + sigma[j]
    earlier = running
    for hop in (1, 2, 4):
        earlier = earlier + jnp.where(sublane >= hop, pltpu.roll(earlier, hop, 0), 0.0)
    earlier = earlier - running
    weights = []
    for j in range(steps):
        inside = earlier if j == 0 else earlier + before[j]
        shadow = jnp.exp(inside * ratio)
        passed = jnp.exp(sigma[j])
        if ahead[j] is None:
            after = passed
            weights.append((1.0 - passed) * shadow)
        else:
            after = ahead[j] * passed
            weights.append((ahead[j] - after) * shadow)
        ahead[j] = after
    return cells, places, weights


def put_halves(send_ref, keep_ref, sums, tile, bits):
    mine = lax.axis_index("view") & 1
    for q in range(1 << bits - 1):
        octet = 2 * bit_reversed(q, bits - 1)
        for k in range(send_ref.shape[1]):
            send_ref[q, k, tile] = sums[k, pl.ds(octet + 1 - mine, SUB, stride=SUB), :]
            keep_ref[q, k, tile] = sums[k, pl.ds(octet + mine, SUB, stride=SUB), :]


def shade_kernel(
    ratio, knots, first, total, bits, pieces, far, late, whole_out,
    code_ref, tint_ref, coef, *rest,
):
    cell_refs, rest = rest[:2], rest[2:]
    brick_refs = [rest[at * len(pieces) : (at + 1) * len(pieces)] for at in range(far)]
    rest = rest[far * len(pieces) + late :]
    if whole_out:
        out_ref, lighting, sums = rest
    else:
        send_ref, keep_ref, lighting, sums = rest
    layers, slices = cell_refs[0].shape[1:3]
    steps = slices // SUB
    channels = lighting.shape[0]
    fill_lighting(pieces, brick_refs, code_ref, tint_ref, lighting, first, total)

    @pl.loop(0, lighting.shape[2] // LANE)
    def _(tile):
        columns = pl.ds(pl.multiple_of(tile * LANE, LANE), LANE)
        ahead = [None] * steps
        for b in range(layers):
            cells, places, weights = weights_of(
                cell_refs, first // LANE + tile, b, ahead, ratio, knots
            )
            for k in range(channels):
                lit = jnp.broadcast_to(lighting[k, b : b + 1, columns], (SUB, LANE))
                table = [entry * lit for entry in table_of(coef, k + 1)]
                for j in range(steps):
                    rows = pl.ds(j * SUB, SUB)
                    term = value_at(table, places[j], cells[j]) * weights[j]
                    if b == 0:
                        sums[k, rows] = term
                    else:
                        sums[k, rows] = sums[k, rows] + term
        if whole_out:
            for j in range(steps):
                sums[channels, pl.ds(j * SUB, SUB)] = ahead[j]
            for octet in range(SUB):
                for k in range(channels + 1):
                    for part in range(steps // SUB):
                        out_ref[k, tile, pl.ds(octet * steps + part * SUB, SUB)] = sums[
                            k, pl.ds(part * SUB * SUB + octet, SUB, stride=SUB), :
                        ]
        else:
            put_halves(send_ref, keep_ref, sums, tile, bits)


def unlit_kernel(ratio, knots, first, late, coef, *rest):
    cell_refs, out_ref = rest[:2], rest[2 + late]
    tiles, layers, channels, slices, _ = out_ref.shape
    steps = slices // SUB

    @pl.loop(0, tiles)
    def _(tile):
        ahead = [None] * steps
        for b in range(layers):
            cells, places, weights = weights_of(
                cell_refs, first // LANE + tile, b, ahead, ratio, knots
            )
            for k in range(channels):
                table = table_of(coef, k + 1)
                for j in range(steps):
                    term = value_at(table, places[j], cells[j]) * weights[j]
                    out_ref[tile, b, k, j * SUB : j * SUB + SUB] = term


def lit_kernel(first, total, bits, pieces, far, late, code_ref, tint_ref, unlit_ref, *rest):
    brick_refs = [rest[at * len(pieces) : (at + 1) * len(pieces)] for at in range(far)]
    send_ref, keep_ref, lighting, sums = rest[far * len(pieces) + late :]
    tiles, layers, channels, slices, _ = unlit_ref.shape
    fill_lighting(pieces, brick_refs, code_ref, tint_ref, lighting, first, total)

    @pl.loop(0, tiles)
    def _(tile):
        columns = pl.ds(pl.multiple_of(tile * LANE, LANE), LANE)
        for k in range(channels):
            lit = [
                jnp.broadcast_to(lighting[k, b : b + 1, columns], (SUB, LANE))
                for b in range(layers)
            ]
            for j in range(slices // SUB):
                rows = slice(j * SUB, j * SUB + SUB)
                terms = [unlit_ref[tile, b, k, rows] * lit[b] for b in range(layers)]
                sums[k, rows] = functools.reduce(jnp.add, terms)
        put_halves(send_ref, keep_ref, sums, tile, bits)


VMEM = functools.partial(pl.BlockSpec, memory_space=pltpu.VMEM)
SMEM = functools.partial(pl.BlockSpec, memory_space=pltpu.SMEM)
ANY = functools.partial(pl.BlockSpec, memory_space=pl.ANY)
HBM = functools.partial(pl.BlockSpec, memory_space=pltpu.HBM)


def shape(*dims):
    return jax.ShapeDtypeStruct(dims, F32)


def cost(cells, columns, per_cell):
    count = cells.shape[1] * cells.shape[2] * columns
    return pl.CostEstimate(flops=count * per_cell, bytes_accessed=4 * count, transcendentals=0)


MERGE_COST = pl.CostEstimate(flops=2 * 10**10, bytes_accessed=2**20, transcendentals=0)


def sums(density, tables, index, sigma_scale, ratio, bits, split):
    layers, slices, total = density.shape
    tiles = total // LANE
    half = (1 << bits) // 2
    outs = [
        shape(layers, total),
        shape(tiles, layers, slices, LANE),
        shape(tiles, layers, slices, LANE),
        shape(4 * tables.shape[1], SUB, LANE),
    ]
    cells_shape = outs[1]
    scratch = []
    if split:
        outs += [shape(half, tiles, SUB, LANE)] * 2
        scratch.append(pltpu.VMEM((slices // SUB, SUB, LANE), F32))
    scratch.append(pltpu.SemaphoreType.DMA((tiles,)))
    return pl.pallas_call(
        functools.partial(sums_kernel, sigma_scale, ratio, bits, split),
        in_specs=[VMEM(), VMEM(), HBM()],
        out_specs=[VMEM()] * len(outs),
        out_shape=outs,
        scratch_shapes=scratch,
        compiler_params=params(STREAM_LIMIT),
        cost_estimate=cost(cells_shape, total, 4000),
        name="sums",
    )(index, tables, density)


def shade(coef, cells, knots, code, tint, bricks, pieces, low, high, ratio, bits, whole_out, after=()):
    tiles, layers, slices, _ = cells[0].shape
    channels = tint.shape[1]
    half = (1 << bits) // 2
    if whole_out:
        outs = [shape(channels + 1, (high - low) // LANE, slices, LANE)]
    else:
        outs = [shape(half, channels, (high - low) // LANE, SUB, LANE)] * 2
    operands = [row for rows in bricks for row in rows]
    return pl.pallas_call(
        functools.partial(
            shade_kernel, ratio, knots, low, tiles * LANE, bits, pieces, len(bricks), len(after),
            whole_out,
        ),
        in_specs=[SMEM()] * 2 + [VMEM()] * (3 + len(operands)) + [ANY()] * len(after),
        out_specs=[VMEM()] * len(outs),
        out_shape=outs,
        scratch_shapes=[
            pltpu.VMEM((channels, layers, high - low), F32),
            pltpu.VMEM((channels + 1, slices, LANE), F32),
        ],
        compiler_params=params(),
        cost_estimate=cost(cells[0], high - low, 10000),
        name="shade",
    )(code, tint, coef, *cells, *operands, *after)


def unlit(coef, cells, knots, channels, low, high, ratio, after=()):
    layers, slices = cells[0].shape[1:3]
    return pl.pallas_call(
        functools.partial(unlit_kernel, ratio, knots, low, len(after)),
        in_specs=[VMEM()] * 3 + [ANY()] * len(after),
        out_specs=VMEM(),
        out_shape=shape((high - low) // LANE, layers, channels, slices, LANE),
        compiler_params=params(),
        cost_estimate=cost(cells[0], high - low, 10000),
        name="unlit",
    )(coef, *cells, *after)


def lit(cells, code, tint, bricks, pieces, low, high, total, bits, after=()):
    tiles, layers, channels, slices, _ = cells.shape
    half = (1 << bits) // 2
    operands = [row for rows in bricks for row in rows]
    return pl.pallas_call(
        functools.partial(
            lit_kernel, low, total, bits, pieces, len(bricks), len(after)
        ),
        in_specs=[SMEM()] * 2 + [VMEM()] * (1 + len(operands)) + [ANY()] * len(after),
        out_specs=[VMEM()] * 2,
        out_shape=[shape(half, channels, tiles, SUB, LANE)] * 2,
        scratch_shapes=[
            pltpu.VMEM((channels, layers, high - low), F32),
            pltpu.VMEM((channels, slices, LANE), F32),
        ],
        compiler_params=params(),
        name="lit",
    )(code, tint, cells, *operands, *after)


def merge_clear_kernel(bit, own_ref, other_ref, *rest):
    send_ref, keep_ref = rest[-2:]
    half = send_ref.shape[0]
    mine = lax.axis_index("view") >> bit + 1 & 1
    for at in range(half):
        there, here = (1 - mine) * half + at, mine * half + at
        send_ref[at] = own_ref[there] * other_ref[there]
        keep_ref[at] = own_ref[here] * other_ref[here]


def merge_clear(own, other, bit, after=()):
    half = shape(own.shape[0] // 2, *own.shape[1:])
    return pl.pallas_call(
        functools.partial(merge_clear_kernel, bit),
        in_specs=[VMEM()] * 2 + [ANY()] * len(after),
        out_specs=[VMEM()] * 2,
        out_shape=[half] * 2,
        compiler_params=params(),
        cost_estimate=MERGE_COST,
        name="merge_clear",
    )(own, other, *after)


def merge_kernel(bit, start, parts, *refs):
    owns, others = refs[:parts], refs[parts : 2 * parts]
    own_clear_ref, other_clear_ref, *rest = refs[2 * parts :]
    send_ref, keep_ref = rest[-2:]
    half, channels = keep_ref.shape[:2]
    me = lax.axis_index("view")
    mine = me >> bit + 1 & 1

    def merged(fronts, backs, clear_ref):
        offset = 0
        for front_ref, back_ref in zip(fronts, backs):
            count = front_ref.shape[2]
            tiles, to = pl.ds(start + offset, count), pl.ds(offset, count)
            for at in range(half):
                for to_ref, side in ((send_ref, 1 - mine), (keep_ref, mine)):
                    source = side * half + at
                    clear = clear_ref[source, tiles]
                    for k in range(channels):
                        value = front_ref[source, k] + clear * back_ref[source, k]
                        to_ref[at, k, to] = value
            offset += count

    upper = me >> bit & 1 == 1

    @pl.when(upper)
    def _():
        merged(others, owns, other_clear_ref)

    @pl.when(jnp.logical_not(upper))
    def _():
        merged(owns, others, own_clear_ref)


def merge(owns, others, own_clear, other_clear, bit, low, after=()):
    count, channels = owns[0].shape[:2]
    tiles = sum(own.shape[2] for own in owns)
    half = shape(count // 2, channels, tiles, SUB, LANE)
    outs = [half] * 2
    return pl.pallas_call(
        functools.partial(merge_kernel, bit, low // LANE, len(owns)),
        in_specs=[VMEM()] * (2 * len(owns) + 2) + [ANY()] * len(after),
        out_specs=[VMEM()] * len(outs),
        out_shape=outs,
        compiler_params=params(),
        cost_estimate=MERGE_COST,
        name="merge",
    )(*owns, *others, own_clear, other_clear, *after)


def last_kernel(bit, firsts, *refs):
    chunks = len(firsts)
    owns, others = refs[:chunks], refs[chunks : 2 * chunks]
    own_clear_ref, other_clear_ref, image_ref = refs[2 * chunks :]
    channels = owns[0].shape[1]
    upper = lax.axis_index("view") >> bit & 1 == 1

    def merged(swapped):
        for at, first in enumerate(firsts):
            for tile in range(owns[at].shape[2]):
                columns = slice(first + tile * LANE, first + tile * LANE + LANE)
                whole = first // LANE + tile
                clear = (other_clear_ref if swapped else own_clear_ref)[0, whole]
                for k in range(channels):
                    own, other = owns[at][0, k, tile], others[at][0, k, tile]
                    front, back = (other, own) if swapped else (own, other)
                    image_ref[k, :, columns] = front + clear * back

    for tile in range(own_clear_ref.shape[1]):
        columns = slice(tile * LANE, tile * LANE + LANE)
        image_ref[channels, :, columns] = own_clear_ref[0, tile] * other_clear_ref[0, tile]

    @pl.when(upper)
    def _():
        merged(True)

    @pl.when(jnp.logical_not(upper))
    def _():
        merged(False)


def last(owns, others, own_clear, other_clear, bit, firsts, total):
    return pl.pallas_call(
        functools.partial(last_kernel, bit, firsts),
        in_specs=[VMEM()] * (2 * len(owns) + 2),
        out_specs=VMEM(),
        out_shape=shape(owns[0].shape[1] + 1, SUB, total),
        compiler_params=params(),
        name="last",
    )(*owns, *others, own_clear, other_clear)


def swap(block, bit):
    count = lax.axis_size("view")
    return lax.ppermute(block, "view", [(at, at ^ 1 << bit) for at in range(count)])


def from_earlier(leaving):
    count = lax.axis_size("light")
    return [
        lax.ppermute(leaving, "light", [(at, at + apart) for at in range(count - apart)])
        for apart in range(1, count)
    ]


def composite_over(front, back):
    clear = front[-1:]
    return jnp.concatenate([front[:-1] + clear * back[:-1], clear * back[-1:]])


def plain(density, tables, index, light_code, light_tint, sigma_scale, ratio, bits):
    slices, total = density.shape[1:]
    leaving, *cells, coef = sums(density, tables, index, sigma_scale, ratio, 0, False)
    bricks = [[row] for row in from_earlier(leaving)]
    parts = shade(
        coef, cells, tables.shape[2], light_code, light_tint, bricks, [(0, total)], 0, total, ratio,
        0, True,
    )[0]
    rows = slices >> bits
    depth = parts.shape[0]
    current = parts.transpose(0, 2, 1, 3).reshape((depth,) + (2,) * bits + (rows, total))
    current = current.transpose((0,) + tuple(range(bits, 0, -1)) + (bits + 1, bits + 2))
    for bit in range(bits):
        upper = lax.axis_index("view") >> bit & 1 == 1
        first, second = current[:, 0], current[:, 1]
        kept = jnp.where(upper, second, first)
        arrived = swap(jnp.where(upper, first, second), bit)
        current = composite_over(jnp.where(upper, arrived, kept), jnp.where(upper, kept, arrived))
    return current.reshape(depth, rows, total)


PARTS = ((11,), (12,), (9,))


def ranges(total):
    whole = sum(sum(parts) for parts in PARTS)
    result, done = [], 0
    for parts in PARTS:
        result.append([])
        for part in parts:
            low = total * done // (whole * LANE) * LANE
            done += part
            result[-1].append((low, total * done // (whole * LANE) * LANE))
    return result


def local(density, tables, table_index, light_code, light_tint):
    layers, slices, total = density.shape
    views = lax.axis_size("view")
    bits = views.bit_length() - 1
    sigma_scale = -1.0 / (layers * views)
    ratio = layers * views / (slices * lax.axis_size("light"))
    if views * SUB != slices or bits != 3:
        return plain(
            density, tables, table_index, light_code, light_tint, sigma_scale, ratio, bits
        )
    pieces = [(0, total)]
    chunks = ranges(total)
    knots = tables.shape[2]
    leaving, *cells, coef, send, keep = sums(
        density, tables, table_index, sigma_scale, ratio, bits, True
    )
    bricks = [[row] for row in from_earlier(leaving)]
    clear = [(keep, swap(send, 0))]
    send, keep = merge_clear(*clear[0], 0)
    clear.append((keep, swap(send, 1)))
    first = unlit(coef, cells, knots, light_tint.shape[1], *chunks[0][0], ratio, after=(send,))
    done = lit(first, light_code, light_tint, bricks, pieces, *chunks[0][0], total, bits)
    halves = [(done[1], swap(done[0], 0))]
    clear_send, own_clear = merge_clear(*clear[1], 1, after=(done[0],))
    clear.append((own_clear, swap(clear_send, 2)))
    done = clear_send
    state = []

    def forward(after):
        at = len(state) - 1
        settled = state[at - 1][1] if at else clear[2][1]
        send, keep = merge(
            [state[at][0]], [state[at][1]], *clear[1], 1, chunks[at][0][0], after=(after, settled)
        )
        state[at] = (keep, swap(send, 2))
        return send

    for at, parts in enumerate(chunks):
        for number, (low, high) in enumerate(parts):
            if at:
                send, keep = shade(
                    coef, cells, knots, light_code, light_tint, bricks, pieces, low, high, ratio,
                    bits, False, after=(done,),
                )
                halves.append((keep, swap(send, 0)))
                done = send
                if number == 0:
                    done = forward(done)
        send, keep = merge(*zip(*halves), *clear[0], 0, parts[0][0], after=(done,))
        halves = []
        done = send
        state.append((keep, swap(send, 1)))
    forward(done)
    owns, others = zip(*state)
    return last(owns, others, *clear[2], 2, [parts[0][0] for parts in chunks], total)


def solution(mesh):
    return jax.shard_map(
        local,
        mesh=mesh,
        in_specs=(P("view", "light", None), P(), P("light", "view"), P(), P()),
        out_specs=P(None, ("light", "view"), None),
        check_vma=False,
    )
```
